256 devices in a mesh: tp: 128 (over y, x_lo, z, core), dp: 2 (over x_hi).
Axes of the slice: x: 4 (x_hi: 2, x_lo: 2; x = x_hi * 2 + x_lo), y: 4, z: 8, core: 2. Of those that a mesh axis runs over, the one named last changes fastest.
Arguments:
- tokens: bfloat16 [512, 8192], P('dp', 'tp'), parts along dimension 0, may hold values from -6 to 6
- grad_out: bfloat16 [512, 8192], P('dp', 'tp'), parts along dimension 0, may hold values from -6 to 6
- gate_blocks: bfloat16 [8192, 128, 128], P('tp'), may hold values from -0.09375 to 0.09375
- gate_index: int32 [128, 64], P('tp'), may hold values from 0 to 63, as said below
- gate_count: int32 [128], P('tp'), may hold values from 16 to 64, as said below
- up_blocks: bfloat16 [8192, 128, 128], P('tp'), may hold values from -0.09375 to 0.09375
- up_index: int32 [128, 64], P('tp'), may hold values from 0 to 63, as said below
- up_count: int32 [128], P('tp'), may hold values from 16 to 64, as said below
- down_blocks: bfloat16 [8192, 128, 128], P('tp'), may hold values from -0.0625 to 0.0625
- down_index: int32 [128, 64], P('tp'), may hold values from 0 to 63, as said below
- down_count: int32 [128], P('tp'), may hold values from 16 to 64, as said below
Outputs:
- outputs: bfloat16 [512, 8192], P('dp', 'tp'), parts along dimension 0
- grad_tokens: bfloat16 [512, 8192], P('dp', 'tp'), parts along dimension 0
The draws below stay inside these ranges and needn't reach their ends.
There are 2 independent parts, one for each index of `dp`. The reference program is written for one: setup_inputs(seed, part) draws one part's arguments, and reference() takes and returns one part's arrays. A program takes and returns all parts, laid end to end along the dimension named above; an argument that names none is the same for every part. Nothing has to cross between parts.
Inputs may be any that keep to these rules, and one draw needn't show every extreme that they name: `gate_index`: each row is an ordering of the 64 block rows; entries at positions from gate_count onward are ignored. `gate_count`: both ends occur. `up_index`: each row is an ordering of the 64 block rows; entries at positions from up_count onward are ignored. `up_count`: both ends occur. `down_index`: each row is an ordering of the 64 block columns; entries at positions from down_count onward are ignored. `down_count`: both ends occur.
All inputs are finite; a program needn't handle non-finite values.
Results may differ from the reference program's by a relative error of at most 0.005.
Values may be sent and summed in bfloat16 or wider, within the bound.
No kernel may reach another device: no remote copies, remote signals or barrier semaphores. Data moves between devices by JAX's collectives and lax.ppermute only.
A program may use at most 128 MiB of HBM per device.

```python
import jax
import jax.numpy as jnp

D = 8192
FF = 16384
BLK = 128
TOKENS = 256
SLOTS = 64
HBLK = 128


def layout(key, marker):
    base = jax.random.fold_in(key, marker)
    first, second, third = jax.random.split(base, 3)
    counts = jax.random.randint(first, (HBLK,), SLOTS // 4, 3 * SLOTS // 4 + 1)
    order = jax.random.permutation(second, HBLK)
    counts = counts.at[order[0]].set(SLOTS).at[order[1]].set(SLOTS // 4)
    orders = jax.vmap(lambda single: jax.random.permutation(single, SLOTS))(jax.random.split(third, HBLK))
    return (orders.astype(jnp.int32), counts.astype(jnp.int32))


def draw_gate_index(key, part):
    return layout(key, 11)[0]


def draw_gate_count(key, part):
    return layout(key, 11)[1]


def draw_up_index(key, part):
    return layout(key, 12)[0]


def draw_up_count(key, part):
    return layout(key, 12)[1]


def draw_down_index(key, part):
    return layout(key, 13)[0]


def draw_down_count(key, part):
    return layout(key, 13)[1]


def block_scale(stream_key, shape, shards, least, high):
    def one(dim, shards_of):
        heights = jax.random.uniform(jax.random.fold_in(jax.random.fold_in(stream_key, 6), dim), (shards_of,), jnp.float32, least / len(shards), high / len(shards))
        return jnp.repeat(jnp.exp(heights), shape[dim] // shards_of).reshape((-1,) + (1,) * (len(shape) - dim - 1))

    level = one(*shards[0])
    for cut in shards[1:]:
        level = level * one(*cut)
    return level


def normal_values(key, extent, spread, limit, cuts=(), held_as=jnp.bfloat16):
    gain = block_scale(key, extent, cuts, -0.22, 0.18) if cuts else 1.0
    drawn = jax.random.normal(key, extent, jnp.float32) * spread * gain
    return jnp.minimum(jnp.maximum(drawn, -limit), limit).astype(held_as)


def setup_inputs(seed: int = 0, part: int = 0) -> dict:
    seeds = jax.random.split(jax.random.key(seed), 12)
    part_keys = jax.random.split(jax.random.fold_in(seeds[11], part), 12)
    return {
        "tokens": normal_values(part_keys[0], (TOKENS, D), 1.0, 6.0, ((1, 128),)),
        "grad_out": normal_values(part_keys[1], (TOKENS, D), 1.0, 6.0, ((1, 128),)),
        "gate_blocks": normal_values(seeds[2], (HBLK * SLOTS, BLK, BLK), (D // 2) ** -0.5, 0.09375, ((0, 128),)),
        "gate_index": draw_gate_index(jax.random.fold_in(seeds[11], 71), part),
        "gate_count": draw_gate_count(jax.random.fold_in(seeds[11], 71), part),
        "up_blocks": normal_values(seeds[5], (HBLK * SLOTS, BLK, BLK), (D // 2) ** -0.5, 0.09375, ((0, 128),)),
        "up_index": draw_up_index(jax.random.fold_in(seeds[11], 71), part),
        "up_count": draw_up_count(jax.random.fold_in(seeds[11], 71), part),
        "down_blocks": normal_values(seeds[8], (HBLK * SLOTS, BLK, BLK), (FF // 2) ** -0.5, 0.0625, ((0, 128),)),
        "down_index": draw_down_index(jax.random.fold_in(seeds[11], 71), part),
        "down_count": draw_down_count(jax.random.fold_in(seeds[11], 71), part),
    }


def expand(blocks, index, count):
    live = jnp.arange(SLOTS, dtype=jnp.int32)[None, :] < count[:, None]
    kept = jnp.where(live[:, :, None, None], blocks.reshape(HBLK, SLOTS, BLK, BLK), jnp.zeros((), blocks.dtype))
    owners = jnp.broadcast_to(jnp.arange(HBLK, dtype=jnp.int32)[:, None], (HBLK, SLOTS))
    return jnp.zeros_like(kept).at[owners, index.astype(jnp.int32)].set(kept)


def column_matrix(blocks, index, count):
    return expand(blocks, index, count).transpose(1, 2, 0, 3).reshape(D, FF)


def reference(tokens, grad_out, gate_blocks, gate_index, gate_count, up_blocks, up_index, up_count, down_blocks, down_index, down_count):
    gate_weight = column_matrix(gate_blocks, gate_index, gate_count)
    up_weight = column_matrix(up_blocks, up_index, up_count)
    down_weight = expand(down_blocks, down_index, down_count).transpose(0, 2, 1, 3).reshape(FF, D)
    gate = jnp.dot(tokens, gate_weight, preferred_element_type=jnp.float32)
    upper = jnp.dot(tokens, up_weight, preferred_element_type=jnp.float32)
    sigma = jax.nn.sigmoid(gate)
    hidden = (gate * sigma * upper).astype(jnp.bfloat16)
    outputs = jnp.dot(hidden, down_weight, preferred_element_type=jnp.float32).astype(jnp.bfloat16)
    grad_hidden = jnp.dot(grad_out, down_weight.T, preferred_element_type=jnp.float32)
    grad_gate = (grad_hidden * upper * sigma * (1.0 + gate * (1.0 - sigma))).astype(jnp.bfloat16)
    grad_up = (grad_hidden * gate * sigma).astype(jnp.bfloat16)
    total = jnp.dot(grad_gate, gate_weight.T, preferred_element_type=jnp.float32) + jnp.dot(grad_up, up_weight.T, preferred_element_type=jnp.float32)
    return outputs, total.astype(jnp.bfloat16)
```

```python
import jax
import jax.numpy as jnp
from jax import lax
from jax.sharding import PartitionSpec as P

NY, NX, NZ, NC = 4, 2, 8, 2
SIZES = {"y": NY, "x": NX, "z": NZ, "c": NC}
F32 = jnp.float32
BF16 = jnp.bfloat16


def place(y, x, z, c):
    return ((y * NX + x) * NZ + z) * NC + c


def shift(value, axis, step):
    pairs = []
    for y in range(NY):
        for x in range(NX):
            for z in range(NZ):
                for c in range(NC):
                    at = {"y": y, "x": x, "z": z, "c": c}
                    to = dict(at)
                    to[axis] = (at[axis] + step) % SIZES[axis]
                    pairs.append((place(**at), place(**to)))
    return lax.ppermute(value, "tp", pairs)


def ring_gather(value, axis):
    n = SIZES[axis]
    got = {0: [value]}
    up = down = value
    for step in range(1, n // 2):
        up, down = shift(up, axis, 1), shift(down, axis, -1)
        got[n - step], got[step] = [up], [down]
    half = value.shape[0] // 2
    got[n // 2] = [shift(up[:half], axis, 1), shift(down[half:], axis, -1)]
    return jnp.concatenate([piece for k in range(n) for piece in got[k]])


def ring_reduce(parts, axis):
    n = SIZES[axis]
    half = parts[0].shape[0] // 2
    far = parts[n // 2]
    up_far, down_far = shift(far[:half], axis, 1), shift(far[half:], axis, -1)
    up = down = None
    for step in range(n // 2 - 1, 0, -1):
        ahead, behind = parts[step].astype(F32), parts[n - step].astype(F32)
        if up is None:
            up = jnp.concatenate([ahead[:half] + up_far.astype(F32), ahead[half:]])
            down = jnp.concatenate([behind[:half], behind[half:] + down_far.astype(F32)])
        else:
            up, down = ahead + up.astype(F32), behind + down.astype(F32)
        up, down = shift(up.astype(BF16), axis, 1), shift(down.astype(BF16), axis, -1)
    return parts[0].astype(F32) + up.astype(F32) + down.astype(F32)


def direct_reduce(parts, axis):
    total = parts[0]
    for step in range(1, SIZES[axis]):
        total = total + shift(parts[step].astype(BF16), axis, step).astype(F32)
    return total


def densify(blocks, position, count):
    slots = position.shape[0]
    live = lax.broadcasted_iota(jnp.int32, (slots, slots), 0) < count
    places = lax.broadcasted_iota(jnp.int32, (slots, slots), 1)
    onehot = ((position[:, None] == places) & live).astype(BF16)
    return jnp.einsum("sr,sab->rab", onehot, blocks, preferred_element_type=F32).astype(BF16)


def body(
    tokens,
    grad_out,
    gate_blocks,
    gate_index,
    gate_count,
    up_blocks,
    up_index,
    up_count,
    down_blocks,
    down_index,
    down_count,
):
    me = lax.axis_index("tp")
    core = me % NC
    my_z = (me // NC) % NZ
    my_x = (me // (NC * NZ)) % NX
    my_y = me // (NC * NZ * NX)
    first = core == 0

    def relative(index):
        y, x, z = index // (NX * NZ), (index // NZ) % NX, index % NZ
        return (y - my_y) % NY, (x - my_x) % NX, (z - my_z) % NZ

    def by_z(index):
        y, x, z = relative(index)
        return (z * NY + y) * NX + x

    def by_y(index):
        y, x, z = relative(index)
        return (y * NZ + z) * NX + x

    both = jnp.stack([tokens.T, grad_out.T])
    half = both.shape[2] // 2
    low, high = both[:, :, :half], both[:, :, half:]
    own, other = jnp.where(first, low, high), jnp.where(first, high, low)
    other = shift(other, "c", 1)
    both = jnp.concatenate([jnp.where(first, own, other), jnp.where(first, other, own)], axis=1)
    beside = shift(both, "x", 1)
    act = jnp.concatenate([both[0], beside[0]])
    cot = jnp.concatenate([both[1], beside[1]])
    act = ring_gather(ring_gather(act, "y"), "z")
    cot = ring_gather(ring_gather(cot, "z"), "y")

    block = gate_blocks.shape[-1]
    wide = gate_index.shape[1] * block
    gate_w = densify(gate_blocks, by_z(gate_index[0]), gate_count[0]).reshape(wide, block)
    up_w = densify(up_blocks, by_z(up_index[0]), up_count[0]).reshape(wide, block)
    down_w = densify(down_blocks, by_y(down_index[0]), down_count[0])
    down_w = down_w.transpose(1, 0, 2).reshape(block, wide)
    gate_w, up_w, down_w = (
        jnp.concatenate([w, shift(w, "c", 1)], axis=axis)
        for w, axis in ((gate_w, 1), (up_w, 1), (down_w, 0))
    )
    hidden_units = NC * block
    gate_up = jnp.concatenate([gate_w, up_w], axis=1)

    projected = lax.dot_general(gate_up, act, (((0,), (0,)), ((), ())), preferred_element_type=F32)
    gate, upper = projected[:hidden_units], projected[hidden_units:]
    sigma = jax.nn.sigmoid(gate)
    hidden = (gate * sigma * upper).astype(BF16)
    out = lax.dot_general(down_w, hidden, (((0,), (0,)), ((), ())), preferred_element_type=F32).astype(BF16)
    grad_hidden = jnp.dot(down_w, cot, preferred_element_type=F32)
    grad_gate = (grad_hidden * upper * sigma * (1.0 + gate * (1.0 - sigma))).astype(BF16)
    grad_up = (grad_hidden * gate * sigma).astype(BF16)
    back = jnp.dot(gate_up, jnp.concatenate([grad_gate, grad_up]), preferred_element_type=F32).astype(BF16)

    out = ring_reduce(jnp.split(out, NY), "y")
    out = direct_reduce(jnp.split(out, NZ), "z")
    back = ring_reduce(jnp.split(back, NZ), "z")
    back = direct_reduce(jnp.split(back, NY), "y")
    sums = jnp.stack([out, back]).reshape(2, NX, block, half)
    sums = (sums[:, 0] + shift(sums[:, 1], "x", 1)).astype(BF16)
    low, high = sums[:, : block // 2], sums[:, block // 2 :]
    own, other = jnp.where(first, low, high), jnp.where(first, high, low)
    other = shift(other, "c", 1)
    sums = jnp.concatenate([jnp.where(first, own, other), jnp.where(first, other, own)], axis=2)
    return sums[0].T, sums[1].T


def solution(mesh):
    placed = (
        P("dp", "tp"),
        P("dp", "tp"),
        P("tp", None, None),
        P("tp", None),
        P("tp"),
        P("tp", None, None),
        P("tp", None),
        P("tp"),
        P("tp", None, None),
        P("tp", None),
        P("tp"),
    )
    return jax.shard_map(
        body, mesh=mesh, in_specs=placed, out_specs=(P("dp", "tp"), P("dp", "tp")), check_vma=False
    )
```

```python
import jax
import jax.numpy as jnp
from jax import lax
from jax.sharding import PartitionSpec as P

NY, NX, NZ, NC = 4, 2, 8, 2
SIZES = {"y": NY, "x": NX, "z": NZ, "c": NC}
ORDER = {"y": (0, 2, 1, 3), "z": (0, 4, 2, 6, 1, 5, 3, 7)}
F32 = jnp.float32
BF16 = jnp.bfloat16


def place(y, x, z, c):
    return ((y * NX + x) * NZ + z) * NC + c


def shift(value, **steps):
    pairs = []
    for y in range(NY):
        for x in range(NX):
            for z in range(NZ):
                for c in range(NC):
                    at = {"y": y, "x": x, "z": z, "c": c}
                    to = {axis: (k + steps.get(axis, 0)) % SIZES[axis] for axis, k in at.items()}
                    pairs.append((place(**at), place(**to)))
    return lax.ppermute(value, "tp", pairs)


def double_gather(value, axis):
    step = SIZES[axis] // 2
    while step:
        value = jnp.concatenate([value, shift(value, **{axis: -step})])
        step //= 2
    return value


def halve_reduce(terms, axis):
    step = 1
    while step < SIZES[axis]:
        half = terms.shape[0] // 2
        terms = terms[:half] + shift(terms[half:].astype(BF16), **{axis: step}).astype(F32)
        step *= 2
    return terms


def ring_gather(value, axis, split):
    n = SIZES[axis]
    got = {0: [value]}
    up = down = value
    for step in range(1, n // 2):
        up, down = shift(up, **{axis: 1}), shift(down, **{axis: -1})
        got[n - step], got[step] = [up], [down]
    if split:
        half = value.shape[0] // 2
        got[n // 2] = [shift(up[:half], **{axis: 1}), shift(down[half:], **{axis: -1})]
    else:
        got[n // 2] = [shift(up, **{axis: 1})]
    return jnp.concatenate([piece for k in ORDER[axis] for piece in got[k]])


def ring_reduce(part, axis, split):
    n = SIZES[axis]
    far = part(n // 2).astype(BF16)
    half = far.shape[0] // 2
    if split:
        up, down = shift(far[:half], **{axis: 1}), shift(far[half:], **{axis: -1})
    else:
        up, down = None, shift(far, **{axis: -1})
    for step in range(n // 2 - 1, 0, -1):
        ahead, behind = part(step), part(n - step)
        if up is None:
            behind = behind + down.astype(F32)
        elif up.shape != ahead.shape:
            ahead = jnp.concatenate([ahead[:half] + up.astype(F32), ahead[half:]])
            behind = jnp.concatenate([behind[:half], behind[half:] + down.astype(F32)])
        else:
            ahead, behind = ahead + up.astype(F32), behind + down.astype(F32)
        up, down = shift(ahead.astype(BF16), **{axis: 1}), shift(behind.astype(BF16), **{axis: -1})
    return part(0) + up.astype(F32) + down.astype(F32)


def densify(blocks, position, count, form):
    slots = position.shape[0]
    live = lax.broadcasted_iota(jnp.int32, (slots, slots), 0) < count
    places = lax.broadcasted_iota(jnp.int32, (slots, slots), 1)
    onehot = ((position[:, None] == places) & live).astype(BF16)
    return jnp.einsum(form, onehot, blocks, preferred_element_type=F32).astype(BF16)


def body(
    tokens,
    grad_out,
    gate_blocks,
    gate_index,
    gate_count,
    up_blocks,
    up_index,
    up_count,
    down_blocks,
    down_index,
    down_count,
):
    me = lax.axis_index("tp")
    first = me % NC == 0
    my_z = (me // NC) % NZ
    my_x = (me // (NC * NZ)) % NX
    my_y = me // (NC * NZ * NX)

    def ranked(ahead, axis):
        return sum(jnp.where(ahead == k, rank, 0) for rank, k in enumerate(ORDER[axis]))

    def relative(index):
        y, x, z = index // (NX * NZ), (index // NZ) % NX, index % NZ
        return ranked((y - my_y) % NY, "y"), (x - my_x) % NX, ranked((z - my_z) % NZ, "z")

    def by_z(index):
        y, x, z = relative(index)
        return (z * NY + y) * NX + x

    def by_y(index):
        y, x, z = relative(index)
        return (y * NZ + z) * NX + x

    both = jnp.stack([tokens.T, grad_out.T])
    half = both.shape[2] // 2
    low, high = both[:, :, :half], both[:, :, half:]
    own, other = jnp.where(first, low, high), jnp.where(first, high, low)
    from_core, from_x, from_xc = shift(other, c=1), shift(own, x=1), shift(other, x=1, c=1)

    def in_order(mine, theirs):
        return [jnp.where(first, mine, theirs), jnp.where(first, theirs, mine)]

    both = jnp.concatenate(in_order(own, from_core) + in_order(from_x, from_xc), axis=1)
    both, gate_blocks, up_blocks, down_blocks = lax.optimization_barrier(
        (both, gate_blocks, up_blocks, down_blocks)
    )
    act = ring_gather(double_gather(both[0], "y"), "z", False)
    cot = ring_gather(double_gather(both[1], "z"), "y", True)

    block = gate_blocks.shape[-1]
    wide = gate_index.shape[1] * block
    gate_w = densify(gate_blocks, by_z(gate_index[0]), gate_count[0], "sr,sab->rab")
    up_w = densify(up_blocks, by_z(up_index[0]), up_count[0], "sr,sab->rab")
    down_w = densify(down_blocks, by_y(down_index[0]), down_count[0], "sr,sab->arb")
    down_w = down_w.reshape(block, wide)
    gate_up = jnp.concatenate([gate_w.reshape(wide, block), up_w.reshape(wide, block)], axis=1)
    gate_up = jnp.concatenate([gate_up, shift(gate_up, c=1)], axis=1)
    down_w = jnp.concatenate([down_w, shift(down_w, c=1)])

    projected = lax.dot_general(gate_up, act, (((0,), (0,)), ((), ())), preferred_element_type=F32)
    projected = projected.reshape(NC, 2, block, half)
    gate, upper = projected[:, 0], projected[:, 1]
    sigma = jax.nn.sigmoid(gate)
    hidden = (gate * sigma * upper).astype(BF16).reshape(NC * block, half)
    out = lax.dot_general(down_w, hidden, (((0,), (0,)), ((), ())), preferred_element_type=F32)
    grad_hidden = jnp.dot(down_w, cot, preferred_element_type=F32).reshape(NC, block, half)
    grad_gate = (grad_hidden * upper * sigma * (1.0 + gate * (1.0 - sigma))).astype(BF16)
    grad_up = (grad_hidden * gate * sigma).astype(BF16)
    grads = jnp.stack([grad_gate, grad_up], axis=1).reshape(NC * 2 * block, half)
    back = jnp.dot(gate_up, grads, preferred_element_type=F32)

    out = out.reshape(NY, NZ, NX * block, half)
    back = back.reshape(NZ, NY, NX * block, half)

    def out_part(ahead):
        return out[:, ORDER["z"].index(ahead)].reshape(NY * NX * block, half)

    def back_part(ahead):
        return back[:, ORDER["y"].index(ahead)].reshape(NZ * NX * block, half)

    out = halve_reduce(ring_reduce(out_part, "z", False), "y")
    back = halve_reduce(ring_reduce(back_part, "y", True), "z")
    sums = jnp.stack([out, back]).reshape(2, NX, NC, block // 2, half)
    mine = jnp.where(first, sums[:, :, 0], sums[:, :, 1])
    theirs = jnp.where(first, sums[:, :, 1], sums[:, :, 0])
    own = mine[:, 0] + shift(mine[:, 1], x=1)
    other = shift(theirs[:, 0], c=1) + shift(theirs[:, 1], x=1, c=1)
    result = jnp.concatenate(in_order(own, other), axis=2).astype(BF16)
    return result[0].T, result[1].T


def solution(mesh):
    placed = (
        P("dp", "tp"),
        P("dp", "tp"),
        P("tp", None, None),
        P("tp", None),
        P("tp"),
        P("tp", None, None),
        P("tp", None),
        P("tp"),
        P("tp", None, None),
        P("tp", None),
        P("tp"),
    )
    return jax.shard_map(
        body, mesh=mesh, in_specs=placed, out_specs=(P("dp", "tp"), P("dp", "tp")), check_vma=False
    )
```

```python
import jax
import jax.numpy as jnp
from jax import lax
from jax.experimental import pallas as pl
from jax.experimental.pallas import tpu as pltpu
from jax.sharding import PartitionSpec as P

NY, NX, NZ, NC = 4, 2, 8, 2
SIZES = {"y": NY, "x": NX, "z": NZ, "c": NC}
ORDER = {"y": (0, 2, 1, 3), "z": (0, 4, 2, 6, 1, 5, 3, 7)}
F32 = jnp.float32
BF16 = jnp.bfloat16


def place(y, x, z, c):
    return ((y * NX + x) * NZ + z) * NC + c


def shift(value, **steps):
    pairs = []
    for y in range(NY):
        for x in range(NX):
            for z in range(NZ):
                for c in range(NC):
                    at = {"y": y, "x": x, "z": z, "c": c}
                    to = {axis: (k + steps.get(axis, 0)) % SIZES[axis] for axis, k in at.items()}
                    pairs.append((place(**at), place(**to)))
    return lax.ppermute(value, "tp", pairs)


def double_gather(value, axis):
    step = SIZES[axis] // 2
    while step:
        value = jnp.concatenate([value, shift(value, **{axis: -step})])
        step //= 2
    return value


def halve_reduce(terms, axis):
    step = 1
    while step < SIZES[axis]:
        half = terms.shape[0] // 2
        terms = terms[:half] + shift(terms[half:].astype(BF16), **{axis: step}).astype(F32)
        step *= 2
    return terms


def ring_gather(value, axis, split):
    n = SIZES[axis]
    got = {0: [value]}
    up = down = value
    for step in range(1, n // 2):
        up, down = shift(up, **{axis: 1}), shift(down, **{axis: -1})
        got[n - step], got[step] = [up], [down]
    if split:
        half = value.shape[0] // 2
        got[n // 2] = [shift(up[:half], **{axis: 1}), shift(down[half:], **{axis: -1})]
    else:
        got[n // 2] = [shift(up, **{axis: 1})]
    return jnp.concatenate([piece for k in ORDER[axis] for piece in got[k]])


def ring_reduce(part, axis, split):
    n = SIZES[axis]
    far = part(n // 2).astype(BF16)
    half = far.shape[0] // 2
    if split:
        up, down = shift(far[:half], **{axis: 1}), shift(far[half:], **{axis: -1})
    else:
        up, down = None, shift(far, **{axis: -1})
    for step in range(n // 2 - 1, 0, -1):
        ahead, behind = part(step), part(n - step)
        if up is None:
            behind = behind + down.astype(F32)
        elif up.shape != ahead.shape:
            ahead = jnp.concatenate([ahead[:half] + up.astype(F32), ahead[half:]])
            behind = jnp.concatenate([behind[:half], behind[half:] + down.astype(F32)])
        else:
            ahead, behind = ahead + up.astype(F32), behind + down.astype(F32)
        up, down = shift(ahead.astype(BF16), **{axis: 1}), shift(behind.astype(BF16), **{axis: -1})
    return part(0) + up.astype(F32) + down.astype(F32)


BLOCK = 128
SLOTS = NY * NX * NZ
GROUP = 4


def slot_of(position, count):
    slots = position.shape[0]
    number = lax.broadcasted_iota(jnp.int32, (slots, slots), 1)
    places = lax.broadcasted_iota(jnp.int32, (slots, slots), 0)
    here = (position[None, :] == places) & (number < count)
    return jnp.sum(jnp.where(here, number + 1, 0), axis=1) - 1


def read_block(maps_ref, which, blocks_ref, position):
    slot = maps_ref[which * SLOTS + position]
    return jnp.where(slot >= 0, blocks_ref[jnp.maximum(slot, 0)], jnp.zeros((), BF16))


def load_all(weights, held, sems):
    copies = [pltpu.make_async_copy(ref, held.at[n], sems.at[n]) for n, ref in enumerate(weights)]
    for copy in copies:
        copy.start()
    return copies


def forward_kernel(maps_ref, act_ref, g0, u0, g1, u1, d0, d1, proj_ref, *rest):
    *out_refs, held, sems = rest
    copies = load_all((g0, u0, g1, u1, d0, d1), held, sems)
    proj_ref[...] = jnp.zeros_like(proj_ref)
    for copy in copies[:4]:
        copy.wait()

    def project(i, carry):
        spots = [i * GROUP + j for j in range(GROUP)]
        left = jnp.concatenate([act_ref[p] for p in spots], axis=1)
        for n, which in enumerate((0, 1, 3, 4)):
            right = jnp.concatenate([read_block(maps_ref, which, held.at[n], p) for p in spots], axis=0)
            columns = pl.ds(n * BLOCK, BLOCK)
            proj_ref[:, columns] += jnp.dot(left, right, preferred_element_type=F32)
        return carry

    lax.fori_loop(0, SLOTS // GROUP, project, 0)
    hidden = []
    for n in range(2):
        gate = proj_ref[:, pl.ds(2 * n * BLOCK, BLOCK)]
        upper = proj_ref[:, pl.ds((2 * n + 1) * BLOCK, BLOCK)]
        hidden.append((gate * jax.nn.sigmoid(gate) * upper).astype(BF16))
    hidden = jnp.concatenate(hidden, axis=1)
    for copy in copies[4:]:
        copy.wait()

    for rank, out_ref in enumerate(out_refs):

        def emit(i, carry, rank=rank, out_ref=out_ref):
            for j in range(GROUP):
                p = ((i * (GROUP // NX) + j // NX) * NZ + rank) * NX + j % NX
                right = jnp.concatenate(
                    [read_block(maps_ref, 2, held.at[4], p), read_block(maps_ref, 5, held.at[5], p)], axis=0
                )
                term = jnp.dot(hidden, right, preferred_element_type=F32)
                out_ref[i * GROUP + j] = term.astype(out_ref.dtype)
            return carry

        lax.fori_loop(0, NY * NX // GROUP, emit, 0)


def contract_last(left, right):
    return lax.dot_general(left, right, (((1,), (1,)), ((), ())), preferred_element_type=F32)


def backward_kernel(maps_ref, cot_ref, proj_ref, g0, u0, g1, u1, d0, d1, *rest):
    *back_refs, held, total_ref, sems = rest
    copies = load_all((d0, d1, g0, u0, g1, u1), held, sems)
    total_ref[...] = jnp.zeros_like(total_ref)
    for copy in copies[:2]:
        copy.wait()

    def project(i, carry):
        spots = [i * GROUP + j for j in range(GROUP)]
        left = jnp.concatenate([cot_ref[p] for p in spots], axis=1)
        for n, which in enumerate((2, 5)):
            right = jnp.concatenate([read_block(maps_ref, which, held.at[n], p) for p in spots], axis=1)
            total_ref[:, pl.ds(n * BLOCK, BLOCK)] += contract_last(left, right)
        return carry

    lax.fori_loop(0, SLOTS // GROUP, project, 0)
    grads = []
    for n in range(2):
        gate = proj_ref[:, pl.ds(2 * n * BLOCK, BLOCK)]
        upper = proj_ref[:, pl.ds((2 * n + 1) * BLOCK, BLOCK)]
        grad = total_ref[:, pl.ds(n * BLOCK, BLOCK)]
        sigma = jax.nn.sigmoid(gate)
        grads.append((grad * upper * sigma * (1.0 + gate * (1.0 - sigma))).astype(BF16))
        grads.append((grad * gate * sigma).astype(BF16))
    grads = jnp.concatenate(grads, axis=1)
    for copy in copies[2:]:
        copy.wait()

    for rank, back_ref in enumerate(back_refs):

        def emit(i, carry, rank=rank, back_ref=back_ref):
            for j in range(GROUP):
                p = ((i * (GROUP // NX) + j // NX) * NY + rank) * NX + j % NX
                right = jnp.concatenate(
                    [read_block(maps_ref, which, held.at[2 + n], p) for n, which in enumerate((0, 1, 3, 4))],
                    axis=1,
                )
                back_ref[i * GROUP + j] = contract_last(grads, right).astype(back_ref.dtype)
            return carry

        lax.fori_loop(0, NZ * NX // GROUP, emit, 0)


def turn_kernel(out_ref, back_ref, turned_ref):
    for n, ref in enumerate((out_ref, back_ref)):
        for x in range(NX):
            turned_ref[n, x] = ref[x].T


def terms(axis, blocks):
    return tuple(
        jax.ShapeDtypeStruct((blocks, BLOCK, BLOCK), BF16 if k == SIZES[axis] // 2 else F32)
        for k in ORDER[axis]
    )


def call(kernel, outs, scratch, flops, maps, inputs, weights):
    vmem = pl.BlockSpec(memory_space=pltpu.VMEM)
    anywhere = pl.BlockSpec(memory_space=pl.ANY)
    return pl.pallas_call(
        kernel,
        out_shape=outs,
        in_specs=[pl.BlockSpec(memory_space=pltpu.SMEM)] + [vmem] * len(inputs) + [anywhere] * len(weights),
        out_specs=(vmem,) * len(outs),
        scratch_shapes=[
            pltpu.VMEM((len(weights), SLOTS, BLOCK, BLOCK), BF16),
            *scratch,
            pltpu.SemaphoreType.DMA((len(weights),)),
        ],
        cost_estimate=pl.CostEstimate(flops=flops, bytes_accessed=1 << 24, transcendentals=1 << 15),
        compiler_params=pltpu.CompilerParams(vmem_limit_bytes=24 << 20),
    )(maps, *inputs, *weights)


def body(
    tokens,
    grad_out,
    gate_blocks,
    gate_index,
    gate_count,
    up_blocks,
    up_index,
    up_count,
    down_blocks,
    down_index,
    down_count,
):
    me = lax.axis_index("tp")
    first = me % NC == 0
    my_z = (me // NC) % NZ
    my_x = (me // (NC * NZ)) % NX
    my_y = me // (NC * NZ * NX)

    def ranked(ahead, axis):
        return sum(jnp.where(ahead == k, rank, 0) for rank, k in enumerate(ORDER[axis]))

    def relative(index):
        y, x, z = index // (NX * NZ), (index // NZ) % NX, index % NZ
        return ranked((y - my_y) % NY, "y"), (x - my_x) % NX, ranked((z - my_z) % NZ, "z")

    def by_z(index):
        y, x, z = relative(index)
        return (z * NY + y) * NX + x

    def by_y(index):
        y, x, z = relative(index)
        return (y * NZ + z) * NX + x

    both = jnp.stack([tokens.T, grad_out.T])
    half = both.shape[2] // 2
    low, high = both[:, :, :half], both[:, :, half:]
    own, other = jnp.where(first, low, high), jnp.where(first, high, low)
    from_core, from_x, from_xc = shift(other, c=1), shift(own, x=1), shift(other, x=1, c=1)

    def in_order(mine, theirs):
        return [jnp.where(first, mine, theirs), jnp.where(first, theirs, mine)]

    both = jnp.concatenate(in_order(own, from_core) + in_order(from_x, from_xc), axis=1)
    both, gate_blocks, up_blocks, down_blocks = lax.optimization_barrier(
        (both, gate_blocks, up_blocks, down_blocks)
    )
    block = gate_blocks.shape[-1]
    both = both.reshape(2, NX, block, half).swapaxes(2, 3)
    act = ring_gather(double_gather(both[0], "y"), "z", False)
    cot = ring_gather(double_gather(both[1], "z"), "y", True)

    maps = jnp.concatenate(
        [
            slot_of(by_z(gate_index[0]), gate_count[0]),
            slot_of(by_z(up_index[0]), up_count[0]),
            slot_of(by_y(down_index[0]), down_count[0]),
        ]
    )
    maps = jnp.concatenate([maps, shift(maps, c=1)])
    weights = (gate_blocks, up_blocks, shift(gate_blocks, c=1), shift(up_blocks, c=1))
    weights += (down_blocks, shift(down_blocks, c=1))
    flops = 6 * NC * SLOTS * block * block * half
    proj, *out = call(
        forward_kernel,
        (jax.ShapeDtypeStruct((half, 2 * NC * block), F32), *terms("z", NY * NX)),
        [],
        flops,
        maps,
        (act,),
        weights,
    )
    back = call(
        backward_kernel,
        terms("y", NZ * NX),
        [pltpu.VMEM((half, NC * block), F32)],
        flops,
        maps,
        (cot, proj),
        weights,
    )
    out = halve_reduce(ring_reduce(lambda k: out[ORDER["z"].index(k)], "z", False), "y")
    back = halve_reduce(ring_reduce(lambda k: back[ORDER["y"].index(k)], "y", True), "z")
    sums = pl.pallas_call(
        turn_kernel,
        out_shape=jax.ShapeDtypeStruct((2, NX, block, half), F32),
        compiler_params=pltpu.CompilerParams(vmem_limit_bytes=4 << 20),
    )(out, back)
    sums = sums.reshape(2, NX, NC, block // 2, half)
    mine = jnp.where(first, sums[:, :, 0], sums[:, :, 1])
    theirs = jnp.where(first, sums[:, :, 1], sums[:, :, 0])
    own = mine[:, 0] + shift(mine[:, 1], x=1)
    other = shift(theirs[:, 0], c=1) + shift(theirs[:, 1], x=1, c=1)
    result = jnp.concatenate(in_order(own, other), axis=2).astype(BF16)
    return result[0].T, result[1].T


def solution(mesh):
    placed = (
        P("dp", "tp"),
        P("dp", "tp"),
        P("tp", None, None),
        P("tp", None),
        P("tp"),
        P("tp", None, None),
        P("tp", None),
        P("tp"),
        P("tp", None, None),
        P("tp", None),
        P("tp"),
    )
    return jax.shard_map(
        body, mesh=mesh, in_specs=placed, out_specs=(P("dp", "tp"), P("dp", "tp")), check_vma=False
    )
```

```python
import jax
import jax.numpy as jnp
from jax import lax
from jax.experimental import pallas as pl
from jax.experimental.pallas import tpu as pltpu
from jax.sharding import PartitionSpec as P

NY, NX, NZ, NC = 4, 2, 8, 2
SIZES = {"y": NY, "x": NX, "z": NZ, "c": NC}
BLOCK = 128
SLOTS = NY * NX * NZ
RING = 4
PART = SLOTS // RING
GROUP = 4
F32 = jnp.float32
BF16 = jnp.bfloat16


def permute(value, target):
    pairs = []
    for y in range(NY):
        for x in range(NX):
            for z in range(NZ):
                for c in range(NC):
                    at = {"y": y, "x": x, "z": z, "c": c}
                    to = target(dict(at))
                    numbers = [((k["y"] * NX + k["x"]) * NZ + k["z"]) * NC + k["c"] for k in (at, to)]
                    pairs.append(tuple(numbers))
    return lax.ppermute(value, "tp", pairs)


def shift(value, axis, step):
    def target(at):
        at[axis] = (at[axis] + step) % SIZES[axis]
        return at

    return permute(value, target)


def turn(value, axes, step):
    def target(at):
        axis = axes[at["c"]]
        at[axis] = (at[axis] + step) % SIZES[axis]
        return at

    return permute(value, target)


def ring_gather(value, axes):
    half = value.shape[0] // 2
    up, down = turn(value, axes, 1), turn(value, axes, -1)
    far_up, far_down = turn(up[:half], axes, 1), turn(down[half:], axes, -1)
    return jnp.concatenate([value, down, up, far_up, far_down])


def ring_reduce(parts, axes):
    here, ahead, behind, far = parts
    half = here.shape[0] // 2
    far = far.astype(BF16)
    down, up = turn(far[:half], axes, -1), turn(far[half:], axes, 1)
    behind = jnp.concatenate([behind[:half] + down.astype(F32), behind[half:]])
    ahead = jnp.concatenate([ahead[:half], ahead[half:] + up.astype(F32)])
    ahead, behind = turn(ahead.astype(BF16), axes, 1), turn(behind.astype(BF16), axes, -1)
    return here + ahead.astype(F32) + behind.astype(F32)


def read_block(maps_ref, which, blocks_ref, position):
    slot = maps_ref[which * SLOTS + position]
    return jnp.where(slot >= 0, blocks_ref[jnp.maximum(slot, 0)], jnp.zeros((), BF16))


def contract_last(left, right):
    return lax.dot_general(left, right, (((1,), (1,)), ((), ())), preferred_element_type=F32)


def inner_kernel(maps_ref, all_ref, g0, u0, g1, u1, d0, d1, sums_ref):
    core = maps_ref[6 * SLOTS]
    sums_ref[...] = jnp.zeros_like(sums_ref)
    wide = 2 * BLOCK

    def gathered(i):
        spots = [i * GROUP + j for j in range(GROUP)]
        return spots, jnp.concatenate([all_ref[p] for p in spots], axis=1)

    @pl.when(core == 0)
    def _():
        def step(i, carry):
            spots, left = gathered(i)
            for n, pair in enumerate((((0, g0), (1, u0)), ((3, g1), (4, u1)))):
                right = jnp.concatenate(
                    [
                        jnp.concatenate([read_block(maps_ref, k, ref, p) for k, ref in pair], axis=1)
                        for p in spots
                    ],
                    axis=0,
                )
                sums_ref[:, pl.ds(n * wide, wide)] += jnp.dot(left, right, preferred_element_type=F32)
            return carry

        lax.fori_loop(0, SLOTS // GROUP, step, 0, unroll=4)

    @pl.when(core == 1)
    def _():
        def step(i, carry):
            spots, left = gathered(i)
            right = jnp.concatenate(
                [
                    jnp.concatenate([read_block(maps_ref, k, ref, p) for p in spots], axis=1)
                    for k, ref in ((2, d0), (5, d1))
                ],
                axis=0,
            )
            sums_ref[:, pl.ds(0, wide)] += contract_last(left, right)
            return carry

        lax.fori_loop(0, SLOTS // GROUP, step, 0, unroll=4)


def outer_kernel(maps_ref, mine_ref, theirs_ref, g0, u0, g1, u1, d0, d1, *part_refs):
    core = maps_ref[6 * SLOTS]

    def columns(ref, n):
        return ref[:, pl.ds(n * BLOCK, BLOCK)]

    def emit(product):
        for rank, part_ref in enumerate(part_refs):

            def step(i, carry, rank=rank, part_ref=part_ref):
                spots = [i * 2 + j for j in range(2)]
                terms = product([rank * PART + p for p in spots]).astype(part_ref.dtype)
                for j, p in enumerate(spots):
                    part_ref[p] = terms[:, j * BLOCK : (j + 1) * BLOCK]
                return carry

            lax.fori_loop(0, PART // 2, step, 0, unroll=4)

    @pl.when(core == 0)
    def _():
        hidden = []
        for n in range(NC):
            gate, upper = columns(mine_ref, 2 * n), columns(mine_ref, 2 * n + 1)
            hidden.append((gate * jax.nn.sigmoid(gate) * upper).astype(BF16))
        hidden = jnp.concatenate(hidden, axis=1)

        def product(spots):
            right = jnp.concatenate(
                [
                    jnp.concatenate([read_block(maps_ref, k, ref, p) for p in spots], axis=1)
                    for k, ref in ((2, d0), (5, d1))
                ],
                axis=0,
            )
            return jnp.dot(hidden, right, preferred_element_type=F32)

        emit(product)

    @pl.when(core == 1)
    def _():
        grads = []
        for n in range(NC):
            gate, upper = columns(theirs_ref, 2 * (1 - n)), columns(theirs_ref, 2 * (1 - n) + 1)
            grad = columns(mine_ref, n)
            sigma = jax.nn.sigmoid(gate)
            grads.append((grad * upper * sigma * (1.0 + gate * (1.0 - sigma))).astype(BF16))
            grads.append((grad * gate * sigma).astype(BF16))
        grads = jnp.concatenate(grads, axis=1)

        def product(spots):
            right = jnp.concatenate(
                [
                    jnp.concatenate(
                        [read_block(maps_ref, k, ref, p) for k, ref in ((0, g0), (1, u0), (3, g1), (4, u1))],
                        axis=1,
                    )
                    for p in spots
                ],
                axis=0,
            )
            return contract_last(grads, right)

        emit(product)


def transpose_kernel(block_ref, turned_ref):
    turned_ref[...] = block_ref[...].T


def transpose(block):
    return pl.pallas_call(
        transpose_kernel,
        out_shape=jax.ShapeDtypeStruct(block.shape[::-1], block.dtype),
        compiler_params=pltpu.CompilerParams(vmem_limit_bytes=2 << 20),
    )(block)


def call(kernel, outs, flops, maps, *inputs):
    vmem = pl.BlockSpec(memory_space=pltpu.VMEM)
    return pl.pallas_call(
        kernel,
        out_shape=outs,
        in_specs=[pl.BlockSpec(memory_space=pltpu.SMEM)] + [vmem] * len(inputs),
        out_specs=jax.tree.map(lambda _: vmem, outs),
        cost_estimate=pl.CostEstimate(flops=flops, bytes_accessed=1 << 24, transcendentals=1 << 15),
        compiler_params=pltpu.CompilerParams(vmem_limit_bytes=21 << 20),
    )(maps, *inputs)


def body(
    tokens,
    grad_out,
    gate_blocks,
    gate_index,
    gate_count,
    up_blocks,
    up_index,
    up_count,
    down_blocks,
    down_index,
    down_count,
):
    me = lax.axis_index("tp")
    core, my_z, my_x, my_y = me & 1, (me >> 1) & 7, (me >> 4) & 1, me >> 5
    first = core == 0
    batch = tokens.shape[0]

    tokens, grad_out = tokens.T, grad_out.T
    own, other = jnp.where(first, tokens, grad_out), jnp.where(first, grad_out, tokens)
    other = shift(other, "c", 1)
    block = jnp.concatenate([jnp.where(first, own, other), jnp.where(first, other, own)])
    block = transpose(block).reshape(1, batch, BLOCK)
    block = jnp.concatenate([block, shift(block, "z", 4)])
    block = jnp.concatenate([block, shift(block, "x", 1)])
    block = ring_gather(block, "yz")
    block = ring_gather(block, "zy")

    lists = jnp.concatenate([gate_index, up_index, down_index])
    counts = jnp.stack([gate_count, up_count, down_count])
    lists = jnp.concatenate([lists, counts], axis=1)
    lists = jnp.concatenate([lists, shift(lists, "c", 1)])
    index, counts = lists[:, :SLOTS], lists[:, SLOTS:]
    y, x, z = ((index >> 4) - my_y) & 3, ((index >> 3) & 1) ^ my_x, ((index & 7) - my_z) & 7
    low, high = z & 3, z >> 2

    def ranked(k):
        return jnp.where(k >= 2, 5 - k, k)

    y_rank, z_rank = ranked(y), ranked(low)
    from_ahead = jnp.where(first, y_rank >= 2, x == 1)
    flipped = (low == 3) | ((low == 2) & jnp.logical_not(from_ahead))
    high = jnp.where(flipped, 1 - high, high)
    position = jnp.where(first, z_rank * RING + y_rank, y_rank * RING + z_rank) * 4 + x * 2 + high
    number = lax.broadcasted_iota(jnp.int32, (6, SLOTS, SLOTS), 2)
    places = lax.broadcasted_iota(jnp.int32, (6, SLOTS, SLOTS), 1)
    here = (position[:, None, :] == places) & (number < counts[:, :, None])
    maps = jnp.sum(jnp.where(here, number + 1, 0), axis=2) - 1
    maps = jnp.concatenate([maps.reshape(6 * SLOTS), core[None]])

    weights = (gate_blocks, up_blocks, shift(gate_blocks, "c", 1), shift(up_blocks, "c", 1))
    weights += (down_blocks, shift(down_blocks, "c", 1))
    flops = 4 * NC * SLOTS * BLOCK * BLOCK * batch
    mine = call(inner_kernel, jax.ShapeDtypeStruct((batch, 4 * BLOCK), F32), flops, maps, block, *weights)
    theirs = shift(mine, "c", 1)
    parts = tuple(
        jax.ShapeDtypeStruct((PART, batch, BLOCK), BF16 if rank == RING - 1 else F32) for rank in range(RING)
    )
    parts = call(outer_kernel, parts, flops, maps, mine, theirs, *weights)

    total = ring_reduce(parts, "zy")
    total = ring_reduce(jnp.split(total, RING), "yz")
    total = total[:2] + shift(total[2:].astype(BF16), "x", 1).astype(F32)
    total = total[0] + shift(total[1].astype(BF16), "z", 4).astype(F32)
    total = transpose(total).astype(BF16)
    low, high = jnp.split(total, 2)
    own, other = jnp.where(first, low, high), jnp.where(first, high, low)
    other = shift(other, "c", 1)
    return jnp.where(first, own, other).T, jnp.where(first, other, own).T


def solution(mesh):
    placed = (
        P("dp", "tp"),
        P("dp", "tp"),
        P("tp", None, None),
        P("tp", None),
        P("tp"),
        P("tp", None, None),
        P("tp", None),
        P("tp"),
        P("tp", None, None),
        P("tp", None),
        P("tp"),
    )
    return jax.shard_map(
        body, mesh=mesh, in_specs=placed, out_specs=(P("dp", "tp"), P("dp", "tp")), check_vma=False
    )
```

```python
import functools

import jax
import jax.numpy as jnp
from jax import lax
from jax.experimental import pallas as pl
from jax.experimental.pallas import tpu as pltpu
from jax.sharding import PartitionSpec as P

NY, NX, NZ, NC = 4, 2, 8, 2
SIZES = {"y": NY, "x": NX, "z": NZ, "c": NC}
BLOCK = 128
SLOTS = NY * NX * NZ
RING = 4
PIECES = 2 * RING
PART = SLOTS // PIECES
GROUP = 4
F32 = jnp.float32
BF16 = jnp.bfloat16


def permute(value, target):
    pairs = []
    for y in range(NY):
        for x in range(NX):
            for z in range(NZ):
                for c in range(NC):
                    at = {"y": y, "x": x, "z": z, "c": c}
                    to = target(dict(at))
                    numbers = [((k["y"] * NX + k["x"]) * NZ + k["z"]) * NC + k["c"] for k in (at, to)]
                    pairs.append(tuple(numbers))
    return lax.ppermute(value, "tp", pairs)


def shift(value, axis, step):
    def target(at):
        at[axis] = (at[axis] + step) % SIZES[axis]
        return at

    return permute(value, target)


def turn(value, axes, step):
    def target(at):
        axis = axes[at["c"]]
        at[axis] = (at[axis] + step) % SIZES[axis]
        return at

    return permute(value, target)


def near(value):
    far = permute(value, lambda at: at | {"x": 1 - at["x"], "z": (at["z"] + 4) % NZ})
    ahead, beside = shift(value, "z", 4), shift(value, "x", 1)
    return jnp.concatenate([value, ahead, beside, far])


def near_reduce(total):
    sent = total.astype(BF16)
    far = permute(sent[3], lambda at: at | {"x": 1 - at["x"], "z": (at["z"] + 4) % NZ})
    ahead, beside = shift(sent[1], "z", 4), shift(sent[2], "x", 1)
    return total[0] + ahead.astype(F32) + beside.astype(F32) + far.astype(F32)


def small_gather(value, axes):
    half = value.shape[0] // 2
    down, up = turn(value, axes, -1), turn(value, axes, 1)
    far_up, far_down = turn(up[:half], axes, 1), turn(down[half:], axes, -1)
    return jnp.concatenate([value, down]), jnp.concatenate([up, far_up, far_down])


def large_gather(first, second, axes):
    first_up, first_down = turn(first, axes, 1), turn(first, axes, -1)
    second_down, second_up = turn(second, axes, -1), turn(second, axes, 1)
    first_far, second_far = turn(first_up, axes, 1), turn(second_down, axes, -1)
    return first, second, first_down, second_down, first_up, second_up, first_far, second_far


SENT = (False, False, True, False, False, True, True, True)


def large_reduce(parts, axes):
    first, second, first_ahead, second_ahead, first_behind, second_behind, first_far, second_far = parts
    second_far, first_far = turn(second_far, axes, 1), turn(first_far, axes, -1)
    first_ahead, second_behind = turn(first_ahead, axes, 1), turn(second_behind, axes, -1)
    second_ahead = turn((second_ahead + second_far.astype(F32)).astype(BF16), axes, 1)
    first_behind = turn((first_behind + first_far.astype(F32)).astype(BF16), axes, -1)
    first = first + first_ahead.astype(F32) + first_behind.astype(F32)
    second = second + second_ahead.astype(F32) + second_behind.astype(F32)
    return first, second


def small_reduce(first, second, axes):
    here, ahead = jnp.split(first, 2)
    behind, far = jnp.split(second, 2)
    half = here.shape[0] // 2
    far = far.astype(BF16)
    down, up = turn(far[:half], axes, -1), turn(far[half:], axes, 1)
    behind = jnp.concatenate([behind[:half] + down.astype(F32), behind[half:]])
    ahead = jnp.concatenate([ahead[:half], ahead[half:] + up.astype(F32)])
    ahead, behind = turn(ahead.astype(BF16), axes, 1), turn(behind.astype(BF16), axes, -1)
    return here + ahead.astype(F32) + behind.astype(F32)


def read_block(maps_ref, which, blocks_ref, position):
    slot = maps_ref[which * SLOTS + position]
    return jnp.where(slot >= 0, blocks_ref[jnp.maximum(slot, 0)], jnp.zeros((), BF16))


def contract_last(left, right):
    return lax.dot_general(left, right, (((1,), (1,)), ((), ())), preferred_element_type=F32)


def inner_kernel(base, maps_ref, *refs):
    *piece_refs, g0, u0, g1, u1, d0, d1, sums_ref = refs
    core = maps_ref[6 * SLOTS]
    wide = 2 * BLOCK
    if base:
        start_ref, *piece_refs = piece_refs
        sums_ref[...] = start_ref[...]
    else:
        sums_ref[...] = jnp.zeros_like(sums_ref)

    def groups():
        for rank, ref in enumerate(piece_refs):
            for i in range(0, PART, GROUP):
                spots = [(base + rank) * PART + i + j for j in range(GROUP)]
                yield spots, jnp.concatenate([ref[i + j] for j in range(GROUP)], axis=1)

    @pl.when(core == 0)
    def _():
        for spots, left in groups():
            for n, pair in enumerate((((0, g0), (1, u0)), ((3, g1), (4, u1)))):
                right = jnp.concatenate(
                    [
                        jnp.concatenate([read_block(maps_ref, k, ref, p) for k, ref in pair], axis=1)
                        for p in spots
                    ],
                    axis=0,
                )
                sums_ref[:, pl.ds(n * wide, wide)] += jnp.dot(left, right, preferred_element_type=F32)

    @pl.when(core == 1)
    def _():
        for spots, left in groups():
            right = jnp.concatenate(
                [
                    jnp.concatenate([read_block(maps_ref, k, ref, p) for p in spots], axis=1)
                    for k, ref in ((2, d0), (5, d1))
                ],
                axis=0,
            )
            sums_ref[:, pl.ds(0, wide)] += contract_last(left, right)


def outer_kernel(maps_ref, mine_ref, theirs_ref, g0, u0, g1, u1, d0, d1, *part_refs):
    core = maps_ref[6 * SLOTS]

    def columns(ref, n):
        return ref[:, pl.ds(n * BLOCK, BLOCK)]

    def emit(product):
        for rank, part_ref in enumerate(part_refs):

            def step(i, carry, rank=rank, part_ref=part_ref):
                spots = [i * 2 + j for j in range(2)]
                terms = product([rank * PART + p for p in spots]).astype(part_ref.dtype)
                for j, p in enumerate(spots):
                    part_ref[p] = terms[:, j * BLOCK : (j + 1) * BLOCK]
                return carry

            lax.fori_loop(0, PART // 2, step, 0, unroll=4)

    @pl.when(core == 0)
    def _():
        hidden = []
        for n in range(NC):
            gate, upper = columns(mine_ref, 2 * n), columns(mine_ref, 2 * n + 1)
            hidden.append((gate * jax.nn.sigmoid(gate) * upper).astype(BF16))
        hidden = jnp.concatenate(hidden, axis=1)

        def product(spots):
            right = jnp.concatenate(
                [
                    jnp.concatenate([read_block(maps_ref, k, ref, p) for p in spots], axis=1)
                    for k, ref in ((2, d0), (5, d1))
                ],
                axis=0,
            )
            return jnp.dot(hidden, right, preferred_element_type=F32)

        emit(product)

    @pl.when(core == 1)
    def _():
        grads = []
        for n in range(NC):
            gate, upper = columns(theirs_ref, 2 * (1 - n)), columns(theirs_ref, 2 * (1 - n) + 1)
            grad = columns(mine_ref, n)
            sigma = jax.nn.sigmoid(gate)
            grads.append((grad * upper * sigma * (1.0 + gate * (1.0 - sigma))).astype(BF16))
            grads.append((grad * gate * sigma).astype(BF16))
        grads = jnp.concatenate(grads, axis=1)

        def product(spots):
            right = jnp.concatenate(
                [
                    jnp.concatenate(
                        [read_block(maps_ref, k, ref, p) for k, ref in ((0, g0), (1, u0), (3, g1), (4, u1))],
                        axis=1,
                    )
                    for p in spots
                ],
                axis=0,
            )
            return contract_last(grads, right)

        emit(product)


def transpose_kernel(block_ref, turned_ref):
    turned_ref[...] = block_ref[...].T


def transpose(block):
    return pl.pallas_call(
        transpose_kernel,
        out_shape=jax.ShapeDtypeStruct(block.shape[::-1], block.dtype),
        compiler_params=pltpu.CompilerParams(vmem_limit_bytes=2 << 20),
    )(block)


def call(kernel, outs, flops, maps, *inputs):
    vmem = pl.BlockSpec(memory_space=pltpu.VMEM)
    return pl.pallas_call(
        kernel,
        out_shape=outs,
        in_specs=[pl.BlockSpec(memory_space=pltpu.SMEM)] + [vmem] * len(inputs),
        out_specs=jax.tree.map(lambda _: vmem, outs),
        cost_estimate=pl.CostEstimate(flops=flops, bytes_accessed=1 << 24, transcendentals=1 << 15),
        compiler_params=pltpu.CompilerParams(vmem_limit_bytes=21 << 20),
    )(maps, *inputs)


def body(
    tokens,
    grad_out,
    gate_blocks,
    gate_index,
    gate_count,
    up_blocks,
    up_index,
    up_count,
    down_blocks,
    down_index,
    down_count,
):
    me = lax.axis_index("tp")
    core, my_z, my_x, my_y = me & 1, (me >> 1) & 7, (me >> 4) & 1, me >> 5
    first = core == 0
    batch = tokens.shape[0]

    tokens, grad_out = tokens.T, grad_out.T
    own, other = jnp.where(first, tokens, grad_out), jnp.where(first, grad_out, tokens)
    other = shift(other, "c", 1)
    block = jnp.concatenate([jnp.where(first, own, other), jnp.where(first, other, own)])
    block = transpose(block).reshape(1, batch, BLOCK)
    pieces = large_gather(*small_gather(near(block), "yz"), "zy")

    lists = jnp.concatenate([gate_index, up_index, down_index])
    counts = jnp.stack([gate_count, up_count, down_count])
    lists = jnp.concatenate([lists, counts], axis=1)
    lists = jnp.concatenate([lists, shift(lists, "c", 1)])
    index, counts = lists[:, :SLOTS], lists[:, SLOTS:]
    y, x, z = ((index >> 4) - my_y) & 3, ((index >> 3) & 1) ^ my_x, ((index & 7) - my_z) & 7
    low, high = z & 3, z >> 2

    def ranked(k):
        return jnp.where(k >= 2, 5 - k, k)

    y_rank, z_rank = ranked(y), ranked(low)
    from_ahead = jnp.where(first, y_rank >= 2, x == 1)
    flipped = (low == 3) | ((low == 2) & jnp.logical_not(from_ahead))
    high = jnp.where(flipped, 1 - high, high)
    position = jnp.where(first, z_rank * RING + y_rank, y_rank * RING + z_rank) * 4 + x * 2 + high
    number = lax.broadcasted_iota(jnp.int32, (6, SLOTS, SLOTS), 2)
    places = lax.broadcasted_iota(jnp.int32, (6, SLOTS, SLOTS), 1)
    here = (position[:, None, :] == places) & (number < counts[:, :, None])
    maps = jnp.sum(jnp.where(here, number + 1, 0), axis=2) - 1
    maps = jnp.concatenate([maps.reshape(6 * SLOTS), core[None]])

    weights = (gate_blocks, up_blocks, shift(gate_blocks, "c", 1), shift(up_blocks, "c", 1))
    weights += (down_blocks, shift(down_blocks, "c", 1))
    flops = NC * SLOTS * BLOCK * BLOCK * batch
    sums = jax.ShapeDtypeStruct((batch, 4 * BLOCK), F32)
    mine = call(functools.partial(inner_kernel, 0), sums, 3 * flops, maps, *pieces[:6], *weights)
    mine = call(functools.partial(inner_kernel, 6), sums, flops, maps, mine, *pieces[6:], *weights)
    theirs = shift(mine, "c", 1)
    parts = tuple(jax.ShapeDtypeStruct((PART, batch, BLOCK), BF16 if sent else F32) for sent in SENT)
    parts = call(outer_kernel, parts, 4 * flops, maps, mine, theirs, *weights)
    total = near_reduce(small_reduce(*large_reduce(parts, "zy"), "yz"))
    total = transpose(total).astype(BF16)
    low, high = jnp.split(total, 2)
    own, other = jnp.where(first, low, high), jnp.where(first, high, low)
    other = shift(other, "c", 1)
    return jnp.where(first, own, other).T, jnp.where(first, other, own).T


def solution(mesh):
    placed = (
        P("dp", "tp"),
        P("dp", "tp"),
        P("tp", None, None),
        P("tp", None),
        P("tp"),
        P("tp", None, None),
        P("tp", None),
        P("tp"),
        P("tp", None, None),
        P("tp", None),
        P("tp"),
    )
    return jax.shard_map(
        body, mesh=mesh, in_specs=placed, out_specs=(P("dp", "tp"), P("dp", "tp")), check_vma=False
    )
```

```python
import functools

import jax
import jax.numpy as jnp
from jax import lax
from jax.experimental import pallas as pl
from jax.experimental.pallas import tpu as pltpu
from jax.sharding import PartitionSpec as P

NY, NX, NZ, NC = 4, 2, 8, 2
SIZES = {"y": NY, "x": NX, "z": NZ, "c": NC}
BLOCK = 128
SLOTS = NY * NX * NZ
RING = 4
PIECES = 2 * RING
PART = SLOTS // PIECES
GROUP = 4
F32 = jnp.float32
BF16 = jnp.bfloat16


def permute(value, target):
    pairs = []
    for y in range(NY):
        for x in range(NX):
            for z in range(NZ):
                for c in range(NC):
                    at = {"y": y, "x": x, "z": z, "c": c}
                    to = target(dict(at))
                    numbers = [((k["y"] * NX + k["x"]) * NZ + k["z"]) * NC + k["c"] for k in (at, to)]
                    pairs.append(tuple(numbers))
    return lax.ppermute(value, "tp", pairs)


def shift(value, axis, step):
    def target(at):
        at[axis] = (at[axis] + step) % SIZES[axis]
        return at

    return permute(value, target)


def turn(value, axes, step):
    def target(at):
        axis = axes[at["c"]]
        at[axis] = (at[axis] + step) % SIZES[axis]
        return at

    return permute(value, target)


def small_gather(value, axes):
    up, down = turn(value, axes, 1), turn(value, axes, -1)
    return jnp.concatenate([value, down, up, turn(up, axes, 1)])


def large_gather(first, one, two, axes):
    one_up, one_down = turn(one, axes, 1), turn(one, axes, -1)
    two_up, two_down = turn(two, axes, 1), turn(two, axes, -1)
    far_up, far_down = turn(one_up, axes, 1), turn(jnp.where(first, one_down, two_down), axes, -1)
    return one, two, one_down, two_down, one_up, two_up, far_up, far_down


SENT = (False, False, False, False, False, True, True, True)


def large_reduce(first, parts, axes):
    one, two, one_ahead, two_ahead, one_behind, two_behind, far_behind, far_ahead = parts
    far_ahead, far_behind = turn(far_ahead, axes, 1).astype(F32), turn(far_behind, axes, -1).astype(F32)
    two_behind = turn(two_behind, axes, -1)
    two_ahead = turn((two_ahead + jnp.where(first, 0.0, far_ahead)).astype(BF16), axes, 1)
    one_ahead = turn((one_ahead + jnp.where(first, far_ahead, 0.0)).astype(BF16), axes, 1)
    one_behind = turn((one_behind + far_behind).astype(BF16), axes, -1)
    one = one + one_ahead.astype(F32) + one_behind.astype(F32)
    two = two + two_ahead.astype(F32) + two_behind.astype(F32)
    return one, two


def small_reduce(total, axes):
    here, ahead, behind, far = jnp.split(total, RING)
    ahead, far = turn(ahead.astype(BF16), axes, 1), turn(far.astype(BF16), axes, -1)
    behind = turn((behind + far.astype(F32)).astype(BF16), axes, -1)
    return here + ahead.astype(F32) + behind.astype(F32)


def read_block(maps_ref, which, blocks_ref, position):
    slot = maps_ref[which * SLOTS + position]
    return jnp.where(slot >= 0, blocks_ref[jnp.maximum(slot, 0)], jnp.zeros((), BF16))


def contract_last(left, right):
    return lax.dot_general(left, right, (((1,), (1,)), ((), ())), preferred_element_type=F32)


def inner_kernel(base, maps_ref, *refs):
    *piece_refs, g0, u0, g1, u1, d0, d1, sums_ref = refs
    core = maps_ref[6 * SLOTS]
    wide = 2 * BLOCK
    if base:
        start_ref, *piece_refs = piece_refs
        sums_ref[...] = start_ref[...]
    else:
        sums_ref[...] = jnp.zeros_like(sums_ref)

    def groups():
        for rank, ref in enumerate(piece_refs):
            for i in range(0, PART, GROUP):
                spots = [(base + rank) * PART + i + j for j in range(GROUP)]
                yield spots, jnp.concatenate([ref[i + j] for j in range(GROUP)], axis=1)

    @pl.when(core == 0)
    def _():
        for spots, left in groups():
            for n, pair in enumerate((((0, g0), (1, u0)), ((3, g1), (4, u1)))):
                right = jnp.concatenate(
                    [
                        jnp.concatenate([read_block(maps_ref, k, ref, p) for k, ref in pair], axis=1)
                        for p in spots
                    ],
                    axis=0,
                )
                sums_ref[:, pl.ds(n * wide, wide)] += jnp.dot(left, right, preferred_element_type=F32)

    @pl.when(core == 1)
    def _():
        for spots, left in groups():
            right = jnp.concatenate(
                [
                    jnp.concatenate([read_block(maps_ref, k, ref, p) for p in spots], axis=1)
                    for k, ref in ((2, d0), (5, d1))
                ],
                axis=0,
            )
            sums_ref[:, pl.ds(0, wide)] += contract_last(left, right)


def outer_kernel(maps_ref, mine_ref, theirs_ref, g0, u0, g1, u1, d0, d1, *part_refs):
    core = maps_ref[6 * SLOTS]

    def columns(ref, n):
        return ref[:, pl.ds(n * BLOCK, BLOCK)]

    def emit(product):
        for rank, part_ref in enumerate(part_refs):

            def step(i, carry, rank=rank, part_ref=part_ref):
                spots = [i * 2 + j for j in range(2)]
                terms = product([rank * PART + p for p in spots]).astype(part_ref.dtype)
                for j, p in enumerate(spots):
                    part_ref[p] = terms[:, j * BLOCK : (j + 1) * BLOCK]
                return carry

            lax.fori_loop(0, PART // 2, step, 0, unroll=4)

    @pl.when(core == 0)
    def _():
        hidden = []
        for n in range(NC):
            gate, upper = columns(mine_ref, 2 * n), columns(mine_ref, 2 * n + 1)
            hidden.append((gate * jax.nn.sigmoid(gate) * upper).astype(BF16))
        hidden = jnp.concatenate(hidden, axis=1)

        def product(spots):
            right = jnp.concatenate(
                [
                    jnp.concatenate([read_block(maps_ref, k, ref, p) for p in spots], axis=1)
                    for k, ref in ((2, d0), (5, d1))
                ],
                axis=0,
            )
            return jnp.dot(hidden, right, preferred_element_type=F32)

        emit(product)

    @pl.when(core == 1)
    def _():
        grads = []
        for n in range(NC):
            gate, upper = columns(theirs_ref, 2 * (1 - n)), columns(theirs_ref, 2 * (1 - n) + 1)
            grad = columns(mine_ref, n)
            sigma = jax.nn.sigmoid(gate)
            grads.append((grad * upper * sigma * (1.0 + gate * (1.0 - sigma))).astype(BF16))
            grads.append((grad * gate * sigma).astype(BF16))
        grads = jnp.concatenate(grads, axis=1)

        def product(spots):
            right = jnp.concatenate(
                [
                    jnp.concatenate(
                        [read_block(maps_ref, k, ref, p) for k, ref in ((0, g0), (1, u0), (3, g1), (4, u1))],
                        axis=1,
                    )
                    for p in spots
                ],
                axis=0,
            )
            return contract_last(grads, right)

        emit(product)


def transpose_kernel(block_ref, turned_ref):
    turned_ref[...] = block_ref[...].T


def transpose(block):
    return pl.pallas_call(
        transpose_kernel,
        out_shape=jax.ShapeDtypeStruct(block.shape[::-1], block.dtype),
        compiler_params=pltpu.CompilerParams(vmem_limit_bytes=2 << 20),
    )(block)


def call(kernel, outs, flops, maps, *inputs):
    vmem = pl.BlockSpec(memory_space=pltpu.VMEM)
    return pl.pallas_call(
        kernel,
        out_shape=outs,
        in_specs=[pl.BlockSpec(memory_space=pltpu.SMEM)] + [vmem] * len(inputs),
        out_specs=jax.tree.map(lambda _: vmem, outs),
        cost_estimate=pl.CostEstimate(flops=flops, bytes_accessed=1 << 24, transcendentals=1 << 15),
        compiler_params=pltpu.CompilerParams(vmem_limit_bytes=21 << 20),
    )(maps, *inputs)


def body(
    tokens,
    grad_out,
    gate_blocks,
    gate_index,
    gate_count,
    up_blocks,
    up_index,
    up_count,
    down_blocks,
    down_index,
    down_count,
):
    me = lax.axis_index("tp")
    core, my_z, my_x, my_y = me & 1, (me >> 1) & 7, (me >> 4) & 1, me >> 5
    first = core == 0
    batch = tokens.shape[0]

    tokens, grad_out = tokens.T, grad_out.T
    own, other = jnp.where(first, tokens, grad_out), jnp.where(first, grad_out, tokens)
    other = shift(other, "c", 1)
    block = jnp.concatenate([jnp.where(first, own, other), jnp.where(first, other, own)])
    block = transpose(block).reshape(1, batch, BLOCK)
    one = jnp.concatenate([block, shift(block, "x", 1)])
    two = shift(one, "z", 4)
    pieces = large_gather(first, small_gather(one, "yz"), small_gather(two, "yz"), "zy")

    lists = jnp.concatenate([gate_index, up_index, down_index])
    counts = jnp.stack([gate_count, up_count, down_count])
    lists = jnp.concatenate([lists, counts], axis=1)
    lists = jnp.concatenate([lists, shift(lists, "c", 1)])
    index, counts = lists[:, :SLOTS], lists[:, SLOTS:]
    y, x, z = ((index >> 4) - my_y) & 3, ((index >> 3) & 1) ^ my_x, ((index & 7) - my_z) & 7
    low, high = z & 3, z >> 2

    def ranked(k):
        return jnp.where(k >= 2, 5 - k, k)

    y_rank, z_rank = ranked(y), ranked(low)
    chunk = jnp.where(low >= 2, 1 - high, high)
    large, small = jnp.where(first, z_rank, y_rank), jnp.where(first, y_rank, z_rank)
    position = (large * 2 + chunk) * PART + small * NX + x
    number = lax.broadcasted_iota(jnp.int32, (6, SLOTS, SLOTS), 2)
    places = lax.broadcasted_iota(jnp.int32, (6, SLOTS, SLOTS), 1)
    here = (position[:, None, :] == places) & (number < counts[:, :, None])
    maps = jnp.sum(jnp.where(here, number + 1, 0), axis=2) - 1
    maps = jnp.concatenate([maps.reshape(6 * SLOTS), core[None]])

    weights = (gate_blocks, up_blocks, shift(gate_blocks, "c", 1), shift(up_blocks, "c", 1))
    weights += (down_blocks, shift(down_blocks, "c", 1))
    flops = NC * SLOTS * BLOCK * BLOCK * batch
    sums = jax.ShapeDtypeStruct((batch, 4 * BLOCK), F32)
    mine = call(functools.partial(inner_kernel, 0), sums, 3 * flops, maps, *pieces[:6], *weights)
    mine = call(functools.partial(inner_kernel, 6), sums, flops, maps, mine, *pieces[6:], *weights)
    theirs = shift(mine, "c", 1)
    parts = tuple(jax.ShapeDtypeStruct((PART, batch, BLOCK), BF16 if sent else F32) for sent in SENT)
    parts = call(outer_kernel, parts, 4 * flops, maps, mine, theirs, *weights)
    one, two = large_reduce(first, parts, "zy")
    two = shift(small_reduce(two, "yz").astype(BF16), "z", 4)
    one = small_reduce(one, "yz") + two.astype(F32)
    total = one[0] + shift(one[1].astype(BF16), "x", 1).astype(F32)
    total = transpose(total).astype(BF16)
    low, high = jnp.split(total, 2)
    own, other = jnp.where(first, low, high), jnp.where(first, high, low)
    other = shift(other, "c", 1)
    return jnp.where(first, own, other).T, jnp.where(first, other, own).T


def solution(mesh):
    placed = (
        P("dp", "tp"),
        P("dp", "tp"),
        P("tp", None, None),
        P("tp", None),
        P("tp"),
        P("tp", None, None),
        P("tp", None),
        P("tp"),
        P("tp", None, None),
        P("tp", None),
        P("tp"),
    )
    return jax.shard_map(
        body, mesh=mesh, in_specs=placed, out_specs=(P("dp", "tp"), P("dp", "tp")), check_vma=False
    )
```

```python
import functools

import jax
import jax.numpy as jnp
from jax import lax
from jax.experimental import pallas as pl
from jax.experimental.pallas import tpu as pltpu
from jax.sharding import PartitionSpec as P

NY, NX, NZ, NC = 4, 2, 8, 2
SIZES = {"y": NY, "x": NX, "z": NZ, "c": NC}
BLOCK = 128
SLOTS = NY * NX * NZ
RING = 4
PIECES = 2 * RING
PART = SLOTS // PIECES
GROUP = 4
F32 = jnp.float32
BF16 = jnp.bfloat16


def permute(value, target):
    pairs = []
    for y in range(NY):
        for x in range(NX):
            for z in range(NZ):
                for c in range(NC):
                    at = {"y": y, "x": x, "z": z, "c": c}
                    to = target(dict(at))
                    numbers = [((k["y"] * NX + k["x"]) * NZ + k["z"]) * NC + k["c"] for k in (at, to)]
                    pairs.append(tuple(numbers))
    return lax.ppermute(value, "tp", pairs)


def shift(value, axis, step):
    def target(at):
        at[axis] = (at[axis] + step) % SIZES[axis]
        return at

    return permute(value, target)


def turn(value, axes, step):
    def target(at):
        axis = axes[at["c"]]
        at[axis] = (at[axis] + step) % SIZES[axis]
        return at

    return permute(value, target)


def near(value):
    far = permute(value, lambda at: at | {"x": 1 - at["x"], "z": (at["z"] + 4) % NZ})
    ahead, beside = shift(value, "z", 4), shift(value, "x", 1)
    return jnp.concatenate([value, ahead, beside, far])


def near_reduce(total):
    sent = total.astype(BF16)
    far = permute(sent[3], lambda at: at | {"x": 1 - at["x"], "z": (at["z"] + 4) % NZ})
    ahead, beside = shift(sent[1], "z", 4), shift(sent[2], "x", 1)
    return total[0] + ahead.astype(F32) + beside.astype(F32) + far.astype(F32)


def small_gather(value, axes):
    half = value.shape[0] // 2
    down, up = turn(value, axes, -1), turn(value, axes, 1)
    far_up, far_down = turn(up[:half], axes, 1), turn(down[half:], axes, -1)
    return jnp.concatenate([value, down]), jnp.concatenate([up, far_up, far_down])


def large_gather(first, second, axes):
    first_up, first_down = turn(first, axes, 1), turn(first, axes, -1)
    second_down, second_up = turn(second, axes, -1), turn(second, axes, 1)
    first_far, second_far = turn(first_up, axes, 1), turn(second_down, axes, -1)
    return first, second, first_down, second_down, first_up, second_up, first_far, second_far


SENT = (False, False, True, False, False, True, True, True)


def large_reduce(parts, axes):
    first, second, first_ahead, second_ahead, first_behind, second_behind, first_far, second_far = parts
    second_far, first_far = turn(second_far, axes, 1), turn(first_far, axes, -1)
    first_ahead, second_behind = turn(first_ahead, axes, 1), turn(second_behind, axes, -1)
    second_ahead = turn((second_ahead + second_far.astype(F32)).astype(BF16), axes, 1)
    first_behind = turn((first_behind + first_far.astype(F32)).astype(BF16), axes, -1)
    first = first + first_ahead.astype(F32) + first_behind.astype(F32)
    second = second + second_ahead.astype(F32) + second_behind.astype(F32)
    return first, second


def small_reduce(first, second, axes):
    here, ahead = jnp.split(first, 2)
    behind, far = jnp.split(second, 2)
    half = here.shape[0] // 2
    far = far.astype(BF16)
    down, up = turn(far[:half], axes, -1), turn(far[half:], axes, 1)
    behind = jnp.concatenate([behind[:half] + down.astype(F32), behind[half:]])
    ahead = jnp.concatenate([ahead[:half], ahead[half:] + up.astype(F32)])
    ahead, behind = turn(ahead.astype(BF16), axes, 1), turn(behind.astype(BF16), axes, -1)
    return here + ahead.astype(F32) + behind.astype(F32)


def read_block(maps_ref, which, blocks_ref, position):
    slot = maps_ref[which * SLOTS + position]
    return jnp.where(slot >= 0, blocks_ref[jnp.maximum(slot, 0)], jnp.zeros((), BF16))


def contract_last(left, right):
    return lax.dot_general(left, right, (((1,), (1,)), ((), ())), preferred_element_type=F32)


LOADS = ((0, 1, 2, 3, 4, 5), (4, 5, 0, 1, 2, 3))


def inner_kernel(base, maps_ref, *refs):
    core = maps_ref[6 * SLOTS]
    wide = 2 * BLOCK
    if base:
        start_ref, *piece_refs, held_ref, sums_ref = refs
        sums_ref[...] = start_ref[...]
    else:
        *refs, sums_ref, held_ref, sems = refs
        piece_refs, weight_refs = refs[:-6], refs[-6:]
        copies = [pltpu.make_async_copy(ref, held_ref.at[n], sems.at[n]) for n, ref in enumerate(weight_refs)]
        for k in range(NC):

            @pl.when(core == k)
            def _(k=k):
                for n in LOADS[k]:
                    copies[n].start()

        sums_ref[...] = jnp.zeros_like(sums_ref)
    g0, u0, g1, u1, d0, d1 = (held_ref.at[n] for n in range(6))

    def arrived(ranks):
        if not base:
            for n in ranks:
                copies[n].wait()

    def groups():
        for rank, ref in enumerate(piece_refs):
            for i in range(0, PART, GROUP):
                spots = [(base + rank) * PART + i + j for j in range(GROUP)]
                yield spots, jnp.concatenate([ref[i + j] for j in range(GROUP)], axis=1)

    @pl.when(core == 0)
    def _():
        arrived(LOADS[0][:4])
        for spots, left in groups():
            for n, pair in enumerate((((0, g0), (1, u0)), ((3, g1), (4, u1)))):
                right = jnp.concatenate(
                    [
                        jnp.concatenate([read_block(maps_ref, k, ref, p) for k, ref in pair], axis=1)
                        for p in spots
                    ],
                    axis=0,
                )
                sums_ref[:, pl.ds(n * wide, wide)] += jnp.dot(left, right, preferred_element_type=F32)
        arrived(LOADS[0][4:])

    @pl.when(core == 1)
    def _():
        arrived(LOADS[1][:2])
        for spots, left in groups():
            right = jnp.concatenate(
                [
                    jnp.concatenate([read_block(maps_ref, k, ref, p) for p in spots], axis=1)
                    for k, ref in ((2, d0), (5, d1))
                ],
                axis=0,
            )
            sums_ref[:, pl.ds(0, wide)] += contract_last(left, right)
        arrived(LOADS[1][2:])


def outer_kernel(maps_ref, mine_ref, theirs_ref, held_ref, *part_refs):
    core = maps_ref[6 * SLOTS]
    g0, u0, g1, u1, d0, d1 = (held_ref.at[n] for n in range(6))

    def columns(ref, n):
        return ref[:, pl.ds(n * BLOCK, BLOCK)]

    def emit(product):
        for rank, part_ref in enumerate(part_refs):

            def step(i, carry, rank=rank, part_ref=part_ref):
                spots = [i * 2 + j for j in range(2)]
                terms = product([rank * PART + p for p in spots]).astype(part_ref.dtype)
                for j, p in enumerate(spots):
                    part_ref[p] = terms[:, j * BLOCK : (j + 1) * BLOCK]
                return carry

            lax.fori_loop(0, PART // 2, step, 0, unroll=4)

    @pl.when(core == 0)
    def _():
        hidden = []
        for n in range(NC):
            gate, upper = columns(mine_ref, 2 * n), columns(mine_ref, 2 * n + 1)
            hidden.append((gate * jax.nn.sigmoid(gate) * upper).astype(BF16))
        hidden = jnp.concatenate(hidden, axis=1)

        def product(spots):
            right = jnp.concatenate(
                [
                    jnp.concatenate([read_block(maps_ref, k, ref, p) for p in spots], axis=1)
                    for k, ref in ((2, d0), (5, d1))
                ],
                axis=0,
            )
            return jnp.dot(hidden, right, preferred_element_type=F32)

        emit(product)

    @pl.when(core == 1)
    def _():
        grads = []
        for n in range(NC):
            gate, upper = columns(theirs_ref, 2 * (1 - n)), columns(theirs_ref, 2 * (1 - n) + 1)
            grad = columns(mine_ref, n)
            sigma = jax.nn.sigmoid(gate)
            grads.append((grad * upper * sigma * (1.0 + gate * (1.0 - sigma))).astype(BF16))
            grads.append((grad * gate * sigma).astype(BF16))
        grads = jnp.concatenate(grads, axis=1)

        def product(spots):
            right = jnp.concatenate(
                [
                    jnp.concatenate(
                        [read_block(maps_ref, k, ref, p) for k, ref in ((0, g0), (1, u0), (3, g1), (4, u1))],
                        axis=1,
                    )
                    for p in spots
                ],
                axis=0,
            )
            return contract_last(grads, right)

        emit(product)


def transpose_kernel(block_ref, turned_ref):
    turned_ref[...] = block_ref[...].T


def transpose(block):
    return pl.pallas_call(
        transpose_kernel,
        out_shape=jax.ShapeDtypeStruct(block.shape[::-1], block.dtype),
        compiler_params=pltpu.CompilerParams(vmem_limit_bytes=2 << 20),
    )(block)


def call(kernel, outs, flops, maps, *inputs, weights=()):
    vmem = pl.BlockSpec(memory_space=pltpu.VMEM)
    return pl.pallas_call(
        kernel,
        out_shape=outs,
        in_specs=[pl.BlockSpec(memory_space=pltpu.SMEM)]
        + [vmem] * len(inputs)
        + [pl.BlockSpec(memory_space=pltpu.HBM)] * len(weights),
        out_specs=jax.tree.map(lambda _: vmem, outs),
        scratch_shapes=[pltpu.SemaphoreType.DMA((len(weights),))] if weights else [],
        cost_estimate=pl.CostEstimate(flops=flops, bytes_accessed=1 << 24, transcendentals=1 << 15),
        compiler_params=pltpu.CompilerParams(vmem_limit_bytes=21 << 20),
    )(maps, *inputs, *(pltpu.with_memory_space_constraint(w, pltpu.HBM) for w in weights))


def body(
    tokens,
    grad_out,
    gate_blocks,
    gate_index,
    gate_count,
    up_blocks,
    up_index,
    up_count,
    down_blocks,
    down_index,
    down_count,
):
    me = lax.axis_index("tp")
    core, my_z, my_x, my_y = me & 1, (me >> 1) & 7, (me >> 4) & 1, me >> 5
    first = core == 0
    batch = tokens.shape[0]

    tokens, grad_out = tokens.T, grad_out.T
    own, other = jnp.where(first, tokens, grad_out), jnp.where(first, grad_out, tokens)
    other = shift(other, "c", 1)
    block = jnp.concatenate([jnp.where(first, own, other), jnp.where(first, other, own)])
    block = transpose(block).reshape(1, batch, BLOCK)
    pieces = large_gather(*small_gather(near(block), "yz"), "zy")

    lists = jnp.concatenate([gate_index, up_index, down_index])
    counts = jnp.stack([gate_count, up_count, down_count])
    lists = jnp.concatenate([lists, counts], axis=1)
    lists = jnp.concatenate([lists, shift(lists, "c", 1)])
    index, counts = lists[:, :SLOTS], lists[:, SLOTS:]
    y, x, z = ((index >> 4) - my_y) & 3, ((index >> 3) & 1) ^ my_x, ((index & 7) - my_z) & 7
    low, high = z & 3, z >> 2

    def ranked(k):
        return jnp.where(k >= 2, 5 - k, k)

    y_rank, z_rank = ranked(y), ranked(low)
    from_ahead = jnp.where(first, y_rank >= 2, x == 1)
    flipped = (low == 3) | ((low == 2) & jnp.logical_not(from_ahead))
    high = jnp.where(flipped, 1 - high, high)
    position = jnp.where(first, z_rank * RING + y_rank, y_rank * RING + z_rank) * 4 + x * 2 + high
    number = lax.broadcasted_iota(jnp.int32, (6, SLOTS, SLOTS), 2)
    places = lax.broadcasted_iota(jnp.int32, (6, SLOTS, SLOTS), 1)
    here = (position[:, None, :] == places) & (number < counts[:, :, None])
    maps = jnp.sum(jnp.where(here, number + 1, 0), axis=2) - 1
    maps = jnp.concatenate([maps.reshape(6 * SLOTS), core[None]])

    weights = (gate_blocks, up_blocks, shift(gate_blocks, "c", 1), shift(up_blocks, "c", 1))
    weights += (down_blocks, shift(down_blocks, "c", 1))
    flops = NC * SLOTS * BLOCK * BLOCK * batch
    sums = jax.ShapeDtypeStruct((batch, 4 * BLOCK), F32)
    held = jax.ShapeDtypeStruct((6, SLOTS, BLOCK, BLOCK), BF16)
    mine, held = call(
        functools.partial(inner_kernel, 0), (sums, held), 3 * flops, maps, *pieces[:6], weights=weights
    )
    mine = call(functools.partial(inner_kernel, 6), sums, flops, maps, mine, *pieces[6:], held)
    theirs = shift(mine, "c", 1)
    parts = tuple(jax.ShapeDtypeStruct((PART, batch, BLOCK), BF16 if sent else F32) for sent in SENT)
    parts = call(outer_kernel, parts, 4 * flops, maps, mine, theirs, held)
    total = near_reduce(small_reduce(*large_reduce(parts, "zy"), "yz"))
    total = transpose(total).astype(BF16)
    low, high = jnp.split(total, 2)
    own, other = jnp.where(first, low, high), jnp.where(first, high, low)
    other = shift(other, "c", 1)
    return jnp.where(first, own, other).T, jnp.where(first, other, own).T


def solution(mesh):
    placed = (
        P("dp", "tp"),
        P("dp", "tp"),
        P("tp", None, None),
        P("tp", None),
        P("tp"),
        P("tp", None, None),
        P("tp", None),
        P("tp"),
        P("tp", None, None),
        P("tp", None),
        P("tp"),
    )
    return jax.shard_map(
        body, mesh=mesh, in_specs=placed, out_specs=(P("dp", "tp"), P("dp", "tp")), check_vma=False
    )
```

```python
import functools

import jax
import jax.numpy as jnp
from jax import lax
from jax.experimental import pallas as pl
from jax.experimental.pallas import tpu as pltpu
from jax.sharding import PartitionSpec as P

NY, NX, NZ, NC = 4, 2, 8, 2
SIZES = {"y": NY, "x": NX, "z": NZ, "c": NC}
BLOCK = 128
SLOTS = NY * NX * NZ
RING = 4
PIECES = 2 * RING
PART = SLOTS // PIECES
GROUP = 4
F32 = jnp.float32
BF16 = jnp.bfloat16


def permute(value, target):
    pairs = []
    for y in range(NY):
        for x in range(NX):
            for z in range(NZ):
                for c in range(NC):
                    at = {"y": y, "x": x, "z": z, "c": c}
                    to = target(dict(at))
                    numbers = [((k["y"] * NX + k["x"]) * NZ + k["z"]) * NC + k["c"] for k in (at, to)]
                    pairs.append(tuple(numbers))
    return lax.ppermute(value, "tp", pairs)


def shift(value, axis, step):
    def target(at):
        at[axis] = (at[axis] + step) % SIZES[axis]
        return at

    return permute(value, target)


def turn(value, axes, step):
    def target(at):
        axis = axes[at["c"]]
        at[axis] = (at[axis] + step) % SIZES[axis]
        return at

    return permute(value, target)


def near(value):
    far = permute(value, lambda at: at | {"x": 1 - at["x"], "z": (at["z"] + 4) % NZ})
    ahead, beside = shift(value, "z", 4), shift(value, "x", 1)
    return jnp.concatenate([value, ahead, beside, far])


def near_reduce(total):
    sent = total.astype(BF16)
    far = permute(sent[3], lambda at: at | {"x": 1 - at["x"], "z": (at["z"] + 4) % NZ})
    ahead, beside = shift(sent[1], "z", 4), shift(sent[2], "x", 1)
    return total[0] + ahead.astype(F32) + beside.astype(F32) + far.astype(F32)


def small_gather(value, axes):
    up, down = turn(value, axes, 1), turn(value, axes, -1)
    return jnp.concatenate([value, down, up, turn(up, axes, 1)])


def large_gather(value, axes):
    half = value.shape[0] // 2
    up, down = turn(value, axes, 1), turn(value, axes, -1)
    return value, down, up, turn(up[:half], axes, 1), turn(down[half:], axes, -1)


SENT = (False, False, True, False, False, True, True, True)


def large_reduce(parts, axes):
    first, second, first_ahead, second_ahead, first_behind, second_behind, first_far, second_far = parts
    second_far, first_far = turn(second_far, axes, 1), turn(first_far, axes, -1)
    first_ahead, second_behind = turn(first_ahead, axes, 1), turn(second_behind, axes, -1)
    second_ahead = turn((second_ahead + second_far.astype(F32)).astype(BF16), axes, 1)
    first_behind = turn((first_behind + first_far.astype(F32)).astype(BF16), axes, -1)
    first = first + first_ahead.astype(F32) + first_behind.astype(F32)
    second = second + second_ahead.astype(F32) + second_behind.astype(F32)
    return first, second


def small_reduce(first, second, axes):
    here, ahead = jnp.split(first, 2)
    behind, far = jnp.split(second, 2)
    far = turn(far.astype(BF16), axes, -1)
    ahead = turn(ahead.astype(BF16), axes, 1)
    behind = turn((behind + far.astype(F32)).astype(BF16), axes, -1)
    return here + ahead.astype(F32) + behind.astype(F32)


def read_block(maps_ref, which, blocks_ref, position):
    slot = maps_ref[which * SLOTS + position]
    return jnp.where(slot >= 0, blocks_ref[jnp.maximum(slot, 0)], jnp.zeros((), BF16))


def contract_last(left, right):
    return lax.dot_general(left, right, (((1,), (1,)), ((), ())), preferred_element_type=F32)


LOADS = ((0, 1, 2, 3, 4, 5), (4, 5, 0, 1, 2, 3))


def inner_kernel(base, maps_ref, *refs):
    core = maps_ref[6 * SLOTS]
    wide = 2 * BLOCK
    if base:
        start_ref, *piece_refs, held_ref, sums_ref = refs
        sums_ref[...] = start_ref[...]
    else:
        *refs, sums_ref, held_ref, sems = refs
        piece_refs, weight_refs = refs[:-6], refs[-6:]
        copies = [pltpu.make_async_copy(ref, held_ref.at[n], sems.at[n]) for n, ref in enumerate(weight_refs)]
        for k in range(NC):

            @pl.when(core == k)
            def _(k=k):
                for n in LOADS[k]:
                    copies[n].start()

        sums_ref[...] = jnp.zeros_like(sums_ref)
    g0, u0, g1, u1, d0, d1 = (held_ref.at[n] for n in range(6))

    def arrived(ranks):
        if not base:
            for n in ranks:
                copies[n].wait()

    def groups():
        at = base
        for ref in piece_refs:
            for i in range(0, ref.shape[0], GROUP):
                spots = [at + i + j for j in range(GROUP)]
                yield spots, jnp.concatenate([ref[i + j] for j in range(GROUP)], axis=1)
            at += ref.shape[0]

    @pl.when(core == 0)
    def _():
        arrived(LOADS[0][:4])
        for spots, left in groups():
            for n, pair in enumerate((((0, g0), (1, u0)), ((3, g1), (4, u1)))):
                right = jnp.concatenate(
                    [
                        jnp.concatenate([read_block(maps_ref, k, ref, p) for k, ref in pair], axis=1)
                        for p in spots
                    ],
                    axis=0,
                )
                sums_ref[:, pl.ds(n * wide, wide)] += jnp.dot(left, right, preferred_element_type=F32)
        arrived(LOADS[0][4:])

    @pl.when(core == 1)
    def _():
        arrived(LOADS[1][:2])
        for spots, left in groups():
            right = jnp.concatenate(
                [
                    jnp.concatenate([read_block(maps_ref, k, ref, p) for p in spots], axis=1)
                    for k, ref in ((2, d0), (5, d1))
                ],
                axis=0,
            )
            sums_ref[:, pl.ds(0, wide)] += contract_last(left, right)
        arrived(LOADS[1][2:])


def outer_kernel(maps_ref, mine_ref, theirs_ref, held_ref, *part_refs):
    core = maps_ref[6 * SLOTS]
    g0, u0, g1, u1, d0, d1 = (held_ref.at[n] for n in range(6))

    def columns(ref, n):
        return ref[:, pl.ds(n * BLOCK, BLOCK)]

    def emit(product):
        for rank, part_ref in enumerate(part_refs):

            def step(i, carry, rank=rank, part_ref=part_ref):
                spots = [i * 2 + j for j in range(2)]
                terms = product([rank * PART + p for p in spots]).astype(part_ref.dtype)
                for j, p in enumerate(spots):
                    part_ref[p] = terms[:, j * BLOCK : (j + 1) * BLOCK]
                return carry

            lax.fori_loop(0, PART // 2, step, 0, unroll=4)

    @pl.when(core == 0)
    def _():
        hidden = []
        for n in range(NC):
            gate, upper = columns(mine_ref, 2 * n), columns(mine_ref, 2 * n + 1)
            hidden.append((gate * jax.nn.sigmoid(gate) * upper).astype(BF16))
        hidden = jnp.concatenate(hidden, axis=1)

        def product(spots):
            right = jnp.concatenate(
                [
                    jnp.concatenate([read_block(maps_ref, k, ref, p) for p in spots], axis=1)
                    for k, ref in ((2, d0), (5, d1))
                ],
                axis=0,
            )
            return jnp.dot(hidden, right, preferred_element_type=F32)

        emit(product)

    @pl.when(core == 1)
    def _():
        grads = []
        for n in range(NC):
            gate, upper = columns(theirs_ref, 2 * (1 - n)), columns(theirs_ref, 2 * (1 - n) + 1)
            grad = columns(mine_ref, n)
            sigma = jax.nn.sigmoid(gate)
            grads.append((grad * upper * sigma * (1.0 + gate * (1.0 - sigma))).astype(BF16))
            grads.append((grad * gate * sigma).astype(BF16))
        grads = jnp.concatenate(grads, axis=1)

        def product(spots):
            right = jnp.concatenate(
                [
                    jnp.concatenate(
                        [read_block(maps_ref, k, ref, p) for k, ref in ((0, g0), (1, u0), (3, g1), (4, u1))],
                        axis=1,
                    )
                    for p in spots
                ],
                axis=0,
            )
            return contract_last(grads, right)

        emit(product)


def transpose_kernel(block_ref, turned_ref):
    turned_ref[...] = block_ref[...].T


def transpose(block):
    return pl.pallas_call(
        transpose_kernel,
        out_shape=jax.ShapeDtypeStruct(block.shape[::-1], block.dtype),
        compiler_params=pltpu.CompilerParams(vmem_limit_bytes=2 << 20),
    )(block)


def call(kernel, outs, flops, maps, *inputs, weights=()):
    vmem = pl.BlockSpec(memory_space=pltpu.VMEM)
    return pl.pallas_call(
        kernel,
        out_shape=outs,
        in_specs=[pl.BlockSpec(memory_space=pltpu.SMEM)]
        + [vmem] * len(inputs)
        + [pl.BlockSpec(memory_space=pltpu.HBM)] * len(weights),
        out_specs=jax.tree.map(lambda _: vmem, outs),
        scratch_shapes=[pltpu.SemaphoreType.DMA((len(weights),))] if weights else [],
        cost_estimate=pl.CostEstimate(flops=flops, bytes_accessed=1 << 24, transcendentals=1 << 15),
        compiler_params=pltpu.CompilerParams(vmem_limit_bytes=21 << 20),
    )(maps, *inputs, *(pltpu.with_memory_space_constraint(w, pltpu.HBM) for w in weights))


def body(
    tokens,
    grad_out,
    gate_blocks,
    gate_index,
    gate_count,
    up_blocks,
    up_index,
    up_count,
    down_blocks,
    down_index,
    down_count,
):
    me = lax.axis_index("tp")
    core, my_z, my_x, my_y = me & 1, (me >> 1) & 7, (me >> 4) & 1, me >> 5
    first = core == 0
    batch = tokens.shape[0]

    tokens, grad_out = tokens.T, grad_out.T
    own, other = jnp.where(first, tokens, grad_out), jnp.where(first, grad_out, tokens)
    other = shift(other, "c", 1)
    block = jnp.concatenate([jnp.where(first, own, other), jnp.where(first, other, own)])
    block = transpose(block).reshape(1, batch, BLOCK)
    pieces = large_gather(small_gather(near(block), "yz"), "zy")

    lists = jnp.concatenate([gate_index, up_index, down_index])
    counts = jnp.stack([gate_count, up_count, down_count])
    lists = jnp.concatenate([lists, counts], axis=1)
    lists = jnp.concatenate([lists, shift(lists, "c", 1)])
    index, counts = lists[:, :SLOTS], lists[:, SLOTS:]
    y, x, z = ((index >> 4) - my_y) & 3, ((index >> 3) & 1) ^ my_x, ((index & 7) - my_z) & 7
    low, high = z & 3, z >> 2

    def ranked(k):
        return jnp.where(k >= 2, 5 - k, k)

    y_rank, z_rank = ranked(y), ranked(low)
    from_ahead = first & (y_rank >= 2)
    flipped = (low == 3) | ((low == 2) & jnp.logical_not(from_ahead))
    high = jnp.where(flipped, 1 - high, high)
    position = jnp.where(first, z_rank * RING + y_rank, y_rank * RING + z_rank) * 4 + x * 2 + high
    number = lax.broadcasted_iota(jnp.int32, (6, SLOTS, SLOTS), 2)
    places = lax.broadcasted_iota(jnp.int32, (6, SLOTS, SLOTS), 1)
    here = (position[:, None, :] == places) & (number < counts[:, :, None])
    maps = jnp.sum(jnp.where(here, number + 1, 0), axis=2) - 1
    maps = jnp.concatenate([maps.reshape(6 * SLOTS), core[None]])

    weights = (gate_blocks, up_blocks, shift(gate_blocks, "c", 1), shift(up_blocks, "c", 1))
    weights += (down_blocks, shift(down_blocks, "c", 1))
    flops = NC * SLOTS * BLOCK * BLOCK * batch
    sums = jax.ShapeDtypeStruct((batch, 4 * BLOCK), F32)
    held = jax.ShapeDtypeStruct((6, SLOTS, BLOCK, BLOCK), BF16)
    mine, held = call(
        functools.partial(inner_kernel, 0), (sums, held), 3 * flops, maps, *pieces[:3], weights=weights
    )
    mine = call(functools.partial(inner_kernel, 6 * PART), sums, flops, maps, mine, *pieces[3:], held)
    theirs = shift(mine, "c", 1)
    parts = tuple(jax.ShapeDtypeStruct((PART, batch, BLOCK), BF16 if sent else F32) for sent in SENT)
    parts = call(outer_kernel, parts, 4 * flops, maps, mine, theirs, held)
    total = near_reduce(small_reduce(*large_reduce(parts, "zy"), "yz"))
    total = transpose(total).astype(BF16)
    low, high = jnp.split(total, 2)
    own, other = jnp.where(first, low, high), jnp.where(first, high, low)
    other = shift(other, "c", 1)
    return jnp.where(first, own, other).T, jnp.where(first, other, own).T


def solution(mesh):
    placed = (
        P("dp", "tp"),
        P("dp", "tp"),
        P("tp", None, None),
        P("tp", None),
        P("tp"),
        P("tp", None, None),
        P("tp", None),
        P("tp"),
        P("tp", None, None),
        P("tp", None),
        P("tp"),
    )
    return jax.shard_map(
        body, mesh=mesh, in_specs=placed, out_specs=(P("dp", "tp"), P("dp", "tp")), check_vma=False
    )
```

```python
import functools

import jax
import jax.numpy as jnp
from jax import lax
from jax.experimental import pallas as pl
from jax.experimental.pallas import tpu as pltpu
from jax.sharding import PartitionSpec as P

NY, NX, NZ, NC = 4, 2, 8, 2
SIZES = {"y": NY, "x": NX, "z": NZ, "c": NC}
BLOCK = 128
SLOTS = NY * NX * NZ
RING = 4
PIECES = 2 * RING
PART = SLOTS // PIECES
GROUP = 4
F32 = jnp.float32
BF16 = jnp.bfloat16


def permute(value, target):
    pairs = []
    for y in range(NY):
        for x in range(NX):
            for z in range(NZ):
                for c in range(NC):
                    at = {"y": y, "x": x, "z": z, "c": c}
                    to = target(dict(at))
                    numbers = [((k["y"] * NX + k["x"]) * NZ + k["z"]) * NC + k["c"] for k in (at, to)]
                    pairs.append(tuple(numbers))
    return lax.ppermute(value, "tp", pairs)


def shift(value, axis, step):
    def target(at):
        at[axis] = (at[axis] + step) % SIZES[axis]
        return at

    return permute(value, target)


def turn(value, axes, step):
    def target(at):
        axis = axes[at["c"]]
        at[axis] = (at[axis] + step) % SIZES[axis]
        return at

    return permute(value, target)


def near(value):
    value = jnp.concatenate([value, shift(value, "z", 4)])
    return jnp.concatenate([value, shift(value, "x", 1)])


def near_reduce(total):
    total = total[:2] + shift(total[2:].astype(BF16), "x", 1).astype(F32)
    return total[0] + shift(total[1].astype(BF16), "z", 4).astype(F32)


def small_gather(value, axes):
    up, down = turn(value, axes, 1), turn(value, axes, -1)
    return jnp.concatenate([value, down, up, turn(up, axes, 1)])


def large_gather(value, axes):
    half = value.shape[0] // 2
    up, down = turn(value, axes, 1), turn(value, axes, -1)
    return value, down, up, turn(up[:half], axes, 1), turn(down[half:], axes, -1)


SENT = (False, False, True, False, False, True, True, True)


def large_reduce(parts, axes):
    first, second, first_ahead, second_ahead, first_behind, second_behind, first_far, second_far = parts
    second_far, first_far = turn(second_far, axes, 1), turn(first_far, axes, -1)
    first_ahead, second_behind = turn(first_ahead, axes, 1), turn(second_behind, axes, -1)
    second_ahead = turn((second_ahead + second_far.astype(F32)).astype(BF16), axes, 1)
    first_behind = turn((first_behind + first_far.astype(F32)).astype(BF16), axes, -1)
    first = first + first_ahead.astype(F32) + first_behind.astype(F32)
    second = second + second_ahead.astype(F32) + second_behind.astype(F32)
    return first, second


def small_reduce(first, second, axes):
    here, ahead = jnp.split(first, 2)
    behind, far = jnp.split(second, 2)
    far = turn(far.astype(BF16), axes, -1)
    ahead = turn(ahead.astype(BF16), axes, 1)
    behind = turn((behind + far.astype(F32)).astype(BF16), axes, -1)
    return here + ahead.astype(F32) + behind.astype(F32)


def read_block(maps_ref, which, blocks_ref, position):
    slot = maps_ref[which * SLOTS + position]
    return jnp.where(slot >= 0, blocks_ref[jnp.maximum(slot, 0)], jnp.zeros((), BF16))


def contract_last(left, right):
    return lax.dot_general(left, right, (((1,), (1,)), ((), ())), preferred_element_type=F32)


LOADS = ((0, 1, 2, 3, 4, 5), (4, 5, 0, 1, 2, 3))


def inner_kernel(base, maps_ref, *refs):
    core = maps_ref[6 * SLOTS]
    wide = 2 * BLOCK
    if base:
        start_ref, *piece_refs, held_ref, sums_ref = refs
        sums_ref[...] = start_ref[...]
    else:
        *refs, sums_ref, held_ref, sems = refs
        piece_refs, weight_refs = refs[:-6], refs[-6:]
        copies = [pltpu.make_async_copy(ref, held_ref.at[n], sems.at[n]) for n, ref in enumerate(weight_refs)]
        for k in range(NC):

            @pl.when(core == k)
            def _(k=k):
                for n in LOADS[k]:
                    copies[n].start()

        sums_ref[...] = jnp.zeros_like(sums_ref)
    g0, u0, g1, u1, d0, d1 = (held_ref.at[n] for n in range(6))

    def arrived(ranks):
        if not base:
            for n in ranks:
                copies[n].wait()

    def groups():
        at = base
        for ref in piece_refs:
            for i in range(0, ref.shape[0], GROUP):
                spots = [at + i + j for j in range(GROUP)]
                yield spots, jnp.concatenate([ref[i + j] for j in range(GROUP)], axis=1)
            at += ref.shape[0]

    @pl.when(core == 0)
    def _():
        arrived(LOADS[0][:4])
        for spots, left in groups():
            for n, pair in enumerate((((0, g0), (1, u0)), ((3, g1), (4, u1)))):
                right = jnp.concatenate(
                    [
                        jnp.concatenate([read_block(maps_ref, k, ref, p) for k, ref in pair], axis=1)
                        for p in spots
                    ],
                    axis=0,
                )
                sums_ref[:, pl.ds(n * wide, wide)] += jnp.dot(left, right, preferred_element_type=F32)
        arrived(LOADS[0][4:])

    @pl.when(core == 1)
    def _():
        arrived(LOADS[1][:2])
        for spots, left in groups():
            right = jnp.concatenate(
                [
                    jnp.concatenate([read_block(maps_ref, k, ref, p) for p in spots], axis=1)
                    for k, ref in ((2, d0), (5, d1))
                ],
                axis=0,
            )
            sums_ref[:, pl.ds(0, wide)] += contract_last(left, right)
        arrived(LOADS[1][2:])


def outer_kernel(ranks, maps_ref, mine_ref, theirs_ref, held_ref, *part_refs):
    core = maps_ref[6 * SLOTS]
    g0, u0, g1, u1, d0, d1 = (held_ref.at[n] for n in range(6))

    def columns(ref, n):
        return ref[:, pl.ds(n * BLOCK, BLOCK)]

    def emit(product):
        for rank, part_ref in zip(ranks, part_refs, strict=True):

            def step(i, carry, rank=rank, part_ref=part_ref):
                spots = [i * 2 + j for j in range(2)]
                terms = product([rank * PART + p for p in spots]).astype(part_ref.dtype)
                for j, p in enumerate(spots):
                    part_ref[p] = terms[:, j * BLOCK : (j + 1) * BLOCK]
                return carry

            lax.fori_loop(0, PART // 2, step, 0, unroll=4)

    @pl.when(core == 0)
    def _():
        hidden = []
        for n in range(NC):
            gate, upper = columns(mine_ref, 2 * n), columns(mine_ref, 2 * n + 1)
            hidden.append((gate * jax.nn.sigmoid(gate) * upper).astype(BF16))
        hidden = jnp.concatenate(hidden, axis=1)

        def product(spots):
            right = jnp.concatenate(
                [
                    jnp.concatenate([read_block(maps_ref, k, ref, p) for p in spots], axis=1)
                    for k, ref in ((2, d0), (5, d1))
                ],
                axis=0,
            )
            return jnp.dot(hidden, right, preferred_element_type=F32)

        emit(product)

    @pl.when(core == 1)
    def _():
        grads = []
        for n in range(NC):
            gate, upper = columns(theirs_ref, 2 * (1 - n)), columns(theirs_ref, 2 * (1 - n) + 1)
            grad = columns(mine_ref, n)
            sigma = jax.nn.sigmoid(gate)
            grads.append((grad * upper * sigma * (1.0 + gate * (1.0 - sigma))).astype(BF16))
            grads.append((grad * gate * sigma).astype(BF16))
        grads = jnp.concatenate(grads, axis=1)

        def product(spots):
            right = jnp.concatenate(
                [
                    jnp.concatenate(
                        [read_block(maps_ref, k, ref, p) for k, ref in ((0, g0), (1, u0), (3, g1), (4, u1))],
                        axis=1,
                    )
                    for p in spots
                ],
                axis=0,
            )
            return contract_last(grads, right)

        emit(product)


def transpose_kernel(block_ref, turned_ref):
    turned_ref[...] = block_ref[...].T


def transpose(block):
    return pl.pallas_call(
        transpose_kernel,
        out_shape=jax.ShapeDtypeStruct(block.shape[::-1], block.dtype),
        compiler_params=pltpu.CompilerParams(vmem_limit_bytes=2 << 20),
    )(block)


def call(kernel, outs, flops, maps, *inputs, weights=()):
    vmem = pl.BlockSpec(memory_space=pltpu.VMEM)
    return pl.pallas_call(
        kernel,
        out_shape=outs,
        in_specs=[pl.BlockSpec(memory_space=pltpu.SMEM)]
        + [vmem] * len(inputs)
        + [pl.BlockSpec(memory_space=pltpu.HBM)] * len(weights),
        out_specs=jax.tree.map(lambda _: vmem, outs),
        scratch_shapes=[pltpu.SemaphoreType.DMA((len(weights),))] if weights else [],
        cost_estimate=pl.CostEstimate(flops=flops, bytes_accessed=1 << 24, transcendentals=1 << 15),
        compiler_params=pltpu.CompilerParams(vmem_limit_bytes=21 << 20),
    )(maps, *inputs, *(pltpu.with_memory_space_constraint(w, pltpu.HBM) for w in weights))


def body(
    tokens,
    grad_out,
    gate_blocks,
    gate_index,
    gate_count,
    up_blocks,
    up_index,
    up_count,
    down_blocks,
    down_index,
    down_count,
):
    me = lax.axis_index("tp")
    core, my_z, my_x, my_y = me & 1, (me >> 1) & 7, (me >> 4) & 1, me >> 5
    first = core == 0
    batch = tokens.shape[0]

    tokens, grad_out = tokens.T, grad_out.T
    own, other = jnp.where(first, tokens, grad_out), jnp.where(first, grad_out, tokens)
    other = shift(other, "c", 1)
    block = jnp.concatenate([jnp.where(first, own, other), jnp.where(first, other, own)])
    block = transpose(block).reshape(1, batch, BLOCK)
    pieces = large_gather(small_gather(near(block), "yz"), "zy")

    lists = jnp.concatenate([gate_index, up_index, down_index])
    counts = jnp.stack([gate_count, up_count, down_count])
    lists = jnp.concatenate([lists, counts], axis=1)
    lists = jnp.concatenate([lists, shift(lists, "c", 1)])
    index, counts = lists[:, :SLOTS], lists[:, SLOTS:]
    y, x, z = ((index >> 4) - my_y) & 3, ((index >> 3) & 1) ^ my_x, ((index & 7) - my_z) & 7
    low, high = z & 3, z >> 2

    def ranked(k):
        return jnp.where(k >= 2, 5 - k, k)

    y_rank, z_rank = ranked(y), ranked(low)
    from_ahead = first & (y_rank >= 2)
    flipped = (low == 3) | ((low == 2) & jnp.logical_not(from_ahead))
    high = jnp.where(flipped, 1 - high, high)
    position = jnp.where(first, z_rank * RING + y_rank, y_rank * RING + z_rank) * 4 + x * 2 + high
    number = lax.broadcasted_iota(jnp.int32, (6, SLOTS, SLOTS), 2)
    places = lax.broadcasted_iota(jnp.int32, (6, SLOTS, SLOTS), 1)
    here = (position[:, None, :] == places) & (number < counts[:, :, None])
    maps = jnp.sum(jnp.where(here, number + 1, 0), axis=2) - 1
    maps = jnp.concatenate([maps.reshape(6 * SLOTS), core[None]])

    weights = (gate_blocks, up_blocks, shift(gate_blocks, "c", 1), shift(up_blocks, "c", 1))
    weights += (down_blocks, shift(down_blocks, "c", 1))
    flops = NC * SLOTS * BLOCK * BLOCK * batch
    sums = jax.ShapeDtypeStruct((batch, 4 * BLOCK), F32)
    held = jax.ShapeDtypeStruct((6, SLOTS, BLOCK, BLOCK), BF16)
    mine, held = call(
        functools.partial(inner_kernel, 0), (sums, held), 3 * flops, maps, *pieces[:3], weights=weights
    )
    mine = call(functools.partial(inner_kernel, 6 * PART), sums, flops, maps, mine, *pieces[3:], held)
    theirs = shift(mine, "c", 1)
    parts = [None] * PIECES
    for ranks in ([5, 6, 7], [0, 1, 2, 3, 4]):
        outs = tuple(jax.ShapeDtypeStruct((PART, batch, BLOCK), BF16 if SENT[rank] else F32) for rank in ranks)
        made = call(functools.partial(outer_kernel, ranks), outs, len(ranks) * flops // 2, maps, mine, theirs, held)
        for rank, part in zip(ranks, made, strict=True):
            parts[rank] = part
    total = near_reduce(small_reduce(*large_reduce(parts, "zy"), "yz"))
    total = transpose(total).astype(BF16)
    low, high = jnp.split(total, 2)
    own, other = jnp.where(first, low, high), jnp.where(first, high, low)
    other = shift(other, "c", 1)
    return jnp.where(first, own, other).T, jnp.where(first, other, own).T


def solution(mesh):
    placed = (
        P("dp", "tp"),
        P("dp", "tp"),
        P("tp", None, None),
        P("tp", None),
        P("tp"),
        P("tp", None, None),
        P("tp", None),
        P("tp"),
        P("tp", None, None),
        P("tp", None),
        P("tp"),
    )
    return jax.shard_map(
        body, mesh=mesh, in_specs=placed, out_specs=(P("dp", "tp"), P("dp", "tp")), check_vma=False
    )
```

```python
import functools

import jax
import jax.numpy as jnp
from jax import lax
from jax.experimental import pallas as pl
from jax.experimental.pallas import tpu as pltpu
from jax.sharding import PartitionSpec as P

NY, NX, NZ, NC = 4, 2, 8, 2
SIZES = {"y": NY, "x": NX, "z": NZ, "c": NC}
BLOCK = 128
SLOTS = NY * NX * NZ
RING = 4
PIECES = 2 * RING
PART = SLOTS // PIECES
GROUP = 4
F32 = jnp.float32
BF16 = jnp.bfloat16


def permute(value, target):
    pairs = []
    for y in range(NY):
        for x in range(NX):
            for z in range(NZ):
                for c in range(NC):
                    at = {"y": y, "x": x, "z": z, "c": c}
                    to = target(dict(at))
                    numbers = [((k["y"] * NX + k["x"]) * NZ + k["z"]) * NC + k["c"] for k in (at, to)]
                    pairs.append(tuple(numbers))
    return lax.ppermute(value, "tp", pairs)


def shift(value, axis, step):
    def target(at):
        at[axis] = (at[axis] + step) % SIZES[axis]
        return at

    return permute(value, target)


def turn(value, axes, step):
    def target(at):
        axis = axes[at["c"]]
        at[axis] = (at[axis] + step) % SIZES[axis]
        return at

    return permute(value, target)


def near(value):
    far = permute(value, lambda at: at | {"x": 1 - at["x"], "z": (at["z"] + 4) % NZ})
    ahead, beside = shift(value, "z", 4), shift(value, "x", 1)
    return jnp.concatenate([value, ahead, beside, far])


def near_reduce(total):
    sent = total.astype(BF16)
    far = permute(sent[3], lambda at: at | {"x": 1 - at["x"], "z": (at["z"] + 4) % NZ})
    ahead, beside = shift(sent[1], "z", 4), shift(sent[2], "x", 1)
    return total[0] + ahead.astype(F32) + beside.astype(F32) + far.astype(F32)


def small_gather(value, axes):
    up, down = turn(value, axes, 1), turn(value, axes, -1)
    return jnp.concatenate([value, down, up, turn(up, axes, 1)])


def large_gather(value, axes):
    half = value.shape[0] // 2
    up, down = turn(value, axes, 1), turn(value, axes, -1)
    return value, down, up, turn(up[:half], axes, 1), turn(down[half:], axes, -1)


SENT = (False, False, True, False, False, True, True, True)


def large_reduce(parts, axes):
    first, second, first_ahead, second_ahead, first_behind, second_behind, first_far, second_far = parts
    second_far, first_far = turn(second_far, axes, 1), turn(first_far, axes, -1)
    first_ahead, second_behind = turn(first_ahead, axes, 1), turn(second_behind, axes, -1)
    second_ahead = turn((second_ahead + second_far.astype(F32)).astype(BF16), axes, 1)
    first_behind = turn((first_behind + first_far.astype(F32)).astype(BF16), axes, -1)
    first = first + first_ahead.astype(F32) + first_behind.astype(F32)
    second = second + second_ahead.astype(F32) + second_behind.astype(F32)
    return first, second


def small_reduce(first, second, axes):
    here, ahead = jnp.split(first, 2)
    behind, far = jnp.split(second, 2)
    far = turn(far.astype(BF16), axes, -1)
    ahead = turn(ahead.astype(BF16), axes, 1)
    behind = turn((behind + far.astype(F32)).astype(BF16), axes, -1)
    return here + ahead.astype(F32) + behind.astype(F32)


def read_block(maps_ref, which, blocks_ref, position):
    slot = maps_ref[which * SLOTS + position]
    return jnp.where(slot >= 0, blocks_ref[jnp.maximum(slot, 0)], jnp.zeros((), BF16))


def contract_last(left, right):
    return lax.dot_general(left, right, (((1,), (1,)), ((), ())), preferred_element_type=F32)


LOADS = ((0, 1, 2, 3, 4, 5), (4, 5, 0, 1, 2, 3))


def inner_kernel(base, maps_ref, *refs):
    core = maps_ref[6 * SLOTS]
    wide = 2 * BLOCK
    if base:
        start_ref, *piece_refs, held_ref, sums_ref = refs
        sums_ref[...] = start_ref[...]
    else:
        *refs, sums_ref, held_ref, sems = refs
        piece_refs, weight_refs = refs[:-6], refs[-6:]
        copies = [pltpu.make_async_copy(ref, held_ref.at[n], sems.at[n]) for n, ref in enumerate(weight_refs)]
        for k in range(NC):

            @pl.when(core == k)
            def _(k=k):
                for n in LOADS[k]:
                    copies[n].start()

        sums_ref[...] = jnp.zeros_like(sums_ref)
    g0, u0, g1, u1, d0, d1 = (held_ref.at[n] for n in range(6))

    def arrived(ranks):
        if not base:
            for n in ranks:
                copies[n].wait()

    def groups():
        at = base
        for ref in piece_refs:
            for i in range(0, ref.shape[0], GROUP):
                spots = [at + i + j for j in range(GROUP)]
                yield spots, jnp.concatenate([ref[i + j] for j in range(GROUP)], axis=1)
            at += ref.shape[0]

    @pl.when(core == 0)
    def _():
        arrived(LOADS[0][:4])
        for spots, left in groups():
            for n, pair in enumerate((((0, g0), (1, u0)), ((3, g1), (4, u1)))):
                right = jnp.concatenate(
                    [
                        jnp.concatenate([read_block(maps_ref, k, ref, p) for k, ref in pair], axis=1)
                        for p in spots
                    ],
                    axis=0,
                )
                sums_ref[:, pl.ds(n * wide, wide)] += jnp.dot(left, right, preferred_element_type=F32)
        arrived(LOADS[0][4:])

    @pl.when(core == 1)
    def _():
        arrived(LOADS[1][:2])
        for spots, left in groups():
            right = jnp.concatenate(
                [
                    jnp.concatenate([read_block(maps_ref, k, ref, p) for p in spots], axis=1)
                    for k, ref in ((2, d0), (5, d1))
                ],
                axis=0,
            )
            sums_ref[:, pl.ds(0, wide)] += contract_last(left, right)
        arrived(LOADS[1][2:])


def outer_kernel(maps_ref, mine_ref, theirs_ref, held_ref, *part_refs):
    core = maps_ref[6 * SLOTS]
    g0, u0, g1, u1, d0, d1 = (held_ref.at[n] for n in range(6))

    def columns(ref, n):
        return ref[:, pl.ds(n * BLOCK, BLOCK)]

    def emit(product):
        for rank, part_ref in enumerate(part_refs):

            def step(i, carry, rank=rank, part_ref=part_ref):
                spots = [i * 2 + j for j in range(2)]
                terms = product([rank * PART + p for p in spots]).astype(part_ref.dtype)
                for j, p in enumerate(spots):
                    part_ref[p] = terms[:, j * BLOCK : (j + 1) * BLOCK]
                return carry

            lax.fori_loop(0, PART // 2, step, 0, unroll=4)

    @pl.when(core == 0)
    def _():
        hidden = []
        for n in range(NC):
            gate, upper = columns(mine_ref, 2 * n), columns(mine_ref, 2 * n + 1)
            hidden.append((gate * jax.nn.sigmoid(gate) * upper).astype(BF16))
        hidden = jnp.concatenate(hidden, axis=1)

        def product(spots):
            right = jnp.concatenate(
                [
                    jnp.concatenate([read_block(maps_ref, k, ref, p) for p in spots], axis=1)
                    for k, ref in ((2, d0), (5, d1))
                ],
                axis=0,
            )
            return jnp.dot(hidden, right, preferred_element_type=F32)

        emit(product)

    @pl.when(core == 1)
    def _():
        grads = []
        for n in range(NC):
            gate, upper = columns(theirs_ref, 2 * (1 - n)), columns(theirs_ref, 2 * (1 - n) + 1)
            grad = columns(mine_ref, n)
            sigma = jax.nn.sigmoid(gate)
            grads.append((grad * upper * sigma * (1.0 + gate * (1.0 - sigma))).astype(BF16))
            grads.append((grad * gate * sigma).astype(BF16))
        grads = jnp.concatenate(grads, axis=1)

        def product(spots):
            right = jnp.concatenate(
                [
                    jnp.concatenate(
                        [read_block(maps_ref, k, ref, p) for k, ref in ((0, g0), (1, u0), (3, g1), (4, u1))],
                        axis=1,
                    )
                    for p in spots
                ],
                axis=0,
            )
            return contract_last(grads, right)

        emit(product)


def transpose_kernel(block_ref, turned_ref):
    turned_ref[...] = block_ref[...].T


def transpose(block):
    return pl.pallas_call(
        transpose_kernel,
        out_shape=jax.ShapeDtypeStruct(block.shape[::-1], block.dtype),
        compiler_params=pltpu.CompilerParams(vmem_limit_bytes=2 << 20),
    )(block)


def call(kernel, outs, flops, maps, *inputs, weights=()):
    vmem = pl.BlockSpec(memory_space=pltpu.VMEM)
    return pl.pallas_call(
        kernel,
        out_shape=outs,
        in_specs=[pl.BlockSpec(memory_space=pltpu.SMEM)]
        + [vmem] * len(inputs)
        + [pl.BlockSpec(memory_space=pltpu.HBM)] * len(weights),
        out_specs=jax.tree.map(lambda _: vmem, outs),
        scratch_shapes=[pltpu.SemaphoreType.DMA((len(weights),))] if weights else [],
        cost_estimate=pl.CostEstimate(flops=flops, bytes_accessed=1 << 24, transcendentals=1 << 15),
        compiler_params=pltpu.CompilerParams(vmem_limit_bytes=21 << 20),
    )(maps, *inputs, *(pltpu.with_memory_space_constraint(w, pltpu.HBM) for w in weights))


def body(
    tokens,
    grad_out,
    gate_blocks,
    gate_index,
    gate_count,
    up_blocks,
    up_index,
    up_count,
    down_blocks,
    down_index,
    down_count,
):
    me = lax.axis_index("tp")
    core, my_z, my_x, my_y = me & 1, (me >> 1) & 7, (me >> 4) & 1, me >> 5
    first = core == 0
    batch = tokens.shape[0]

    tokens, grad_out = tokens.T, grad_out.T
    own, other = jnp.where(first, tokens, grad_out), jnp.where(first, grad_out, tokens)
    other = shift(other, "c", 1)
    block = jnp.concatenate([jnp.where(first, own, other), jnp.where(first, other, own)])
    block = transpose(block).reshape(1, batch, BLOCK)
    pieces = large_gather(small_gather(near(block), "zy"), "yz")

    lists = jnp.concatenate([gate_index, up_index, down_index])
    counts = jnp.stack([gate_count, up_count, down_count])
    lists = jnp.concatenate([lists, counts], axis=1)
    lists = jnp.concatenate([lists, shift(lists, "c", 1)])
    index, counts = lists[:, :SLOTS], lists[:, SLOTS:]
    y, x, z = ((index >> 4) - my_y) & 3, ((index >> 3) & 1) ^ my_x, ((index & 7) - my_z) & 7
    low, high = z & 3, z >> 2

    def ranked(k):
        return jnp.where(k >= 2, 5 - k, k)

    y_rank, z_rank = ranked(y), ranked(low)
    z_large = core == 1
    from_ahead = z_large & (y_rank >= 2)
    flipped = (low == 3) | ((low == 2) & jnp.logical_not(from_ahead))
    high = jnp.where(flipped, 1 - high, high)
    position = jnp.where(z_large, z_rank * RING + y_rank, y_rank * RING + z_rank) * 4 + x * 2 + high
    number = lax.broadcasted_iota(jnp.int32, (6, SLOTS, SLOTS), 2)
    places = lax.broadcasted_iota(jnp.int32, (6, SLOTS, SLOTS), 1)
    here = (position[:, None, :] == places) & (number < counts[:, :, None])
    maps = jnp.sum(jnp.where(here, number + 1, 0), axis=2) - 1
    maps = jnp.concatenate([maps.reshape(6 * SLOTS), core[None]])

    weights = (gate_blocks, up_blocks, shift(gate_blocks, "c", 1), shift(up_blocks, "c", 1))
    weights += (down_blocks, shift(down_blocks, "c", 1))
    flops = NC * SLOTS * BLOCK * BLOCK * batch
    sums = jax.ShapeDtypeStruct((batch, 4 * BLOCK), F32)
    held = jax.ShapeDtypeStruct((6, SLOTS, BLOCK, BLOCK), BF16)
    mine, held = call(
        functools.partial(inner_kernel, 0), (sums, held), 3 * flops, maps, *pieces[:3], weights=weights
    )
    mine = call(functools.partial(inner_kernel, 6 * PART), sums, flops, maps, mine, *pieces[3:], held)
    theirs = shift(mine, "c", 1)
    parts = tuple(jax.ShapeDtypeStruct((PART, batch, BLOCK), BF16 if sent else F32) for sent in SENT)
    parts = call(outer_kernel, parts, 4 * flops, maps, mine, theirs, held)
    total = near_reduce(small_reduce(*large_reduce(parts, "yz"), "zy"))
    total = transpose(total).astype(BF16)
    low, high = jnp.split(total, 2)
    own, other = jnp.where(first, low, high), jnp.where(first, high, low)
    other = shift(other, "c", 1)
    return jnp.where(first, own, other).T, jnp.where(first, other, own).T


def solution(mesh):
    placed = (
        P("dp", "tp"),
        P("dp", "tp"),
        P("tp", None, None),
        P("tp", None),
        P("tp"),
        P("tp", None, None),
        P("tp", None),
        P("tp"),
        P("tp", None, None),
        P("tp", None),
        P("tp"),
    )
    return jax.shard_map(
        body, mesh=mesh, in_specs=placed, out_specs=(P("dp", "tp"), P("dp", "tp")), check_vma=False
    )
```

```python
import functools

import jax
import jax.numpy as jnp
from jax import lax
from jax.experimental import pallas as pl
from jax.experimental.pallas import tpu as pltpu
from jax.sharding import PartitionSpec as P

NY, NX, NZ, NC = 4, 2, 8, 2
SIZES = {"y": NY, "x": NX, "z": NZ, "c": NC}
BLOCK = 128
SLOTS = NY * NX * NZ
RING = 4
PIECES = 2 * RING
PART = SLOTS // PIECES
GROUP = 4
F32 = jnp.float32
BF16 = jnp.bfloat16


def permute(value, target):
    pairs = []
    for y in range(NY):
        for x in range(NX):
            for z in range(NZ):
                for c in range(NC):
                    at = {"y": y, "x": x, "z": z, "c": c}
                    to = target(dict(at))
                    numbers = [((k["y"] * NX + k["x"]) * NZ + k["z"]) * NC + k["c"] for k in (at, to)]
                    pairs.append(tuple(numbers))
    return lax.ppermute(value, "tp", pairs)


def shift(value, axis, step):
    def target(at):
        at[axis] = (at[axis] + step) % SIZES[axis]
        return at

    return permute(value, target)


def turn(value, axes, step):
    def target(at):
        axis = axes[at["c"]]
        at[axis] = (at[axis] + step) % SIZES[axis]
        return at

    return permute(value, target)


def near(value):
    far = permute(value, lambda at: at | {"x": 1 - at["x"], "z": (at["z"] + 4) % NZ})
    ahead, beside = shift(value, "z", 4), shift(value, "x", 1)
    return jnp.concatenate([value, ahead, beside, far])


def near_reduce(total):
    sent = total.astype(BF16)
    far = permute(sent[3], lambda at: at | {"x": 1 - at["x"], "z": (at["z"] + 4) % NZ})
    ahead, beside = shift(sent[1], "z", 4), shift(sent[2], "x", 1)
    return total[0] + ahead.astype(F32) + beside.astype(F32) + far.astype(F32)


def small_gather(value, axes):
    up, down = turn(value, axes, 1), turn(value, axes, -1)
    return jnp.concatenate([value, down, up, turn(up, axes, 1)])


def large_gather(value, axes):
    half = value.shape[0] // 2
    up, down = turn(value, axes, 1), turn(value, axes, -1)
    return value, down, up, turn(up[:half], axes, 1), turn(down[half:], axes, -1)


SENT = (False, False, True, False, False, True, True, True)


def large_reduce(parts, axes):
    first, second, first_ahead, second_ahead, first_behind, second_behind, first_far, second_far = parts
    second_far, first_far = turn(second_far, axes, 1), turn(first_far, axes, -1)
    first_ahead, second_behind = turn(first_ahead, axes, 1), turn(second_behind, axes, -1)
    second_ahead = turn((second_ahead + second_far.astype(F32)).astype(BF16), axes, 1)
    first_behind = turn((first_behind + first_far.astype(F32)).astype(BF16), axes, -1)
    first = first + first_ahead.astype(F32) + first_behind.astype(F32)
    second = second + second_ahead.astype(F32) + second_behind.astype(F32)
    return first, second


def small_reduce(first, second, axes):
    here, ahead = jnp.split(first, 2)
    behind, far = jnp.split(second, 2)
    far = turn(far.astype(BF16), axes, -1)
    ahead = turn(ahead.astype(BF16), axes, 1)
    behind = turn((behind + far.astype(F32)).astype(BF16), axes, -1)
    return here + ahead.astype(F32) + behind.astype(F32)


def read_block(maps_ref, which, blocks_ref, position):
    slot = maps_ref[which * SLOTS + position]
    return jnp.where(slot >= 0, blocks_ref[jnp.maximum(slot, 0)], jnp.zeros((), BF16))


def contract_last(left, right):
    return lax.dot_general(left, right, (((1,), (1,)), ((), ())), preferred_element_type=F32)


LOADS = ((0, 1, 2, 3, 4, 5), (4, 5, 0, 1, 2, 3))


def inner_kernel(base, maps_ref, *refs):
    core = maps_ref[6 * SLOTS]
    wide = 2 * BLOCK
    if base:
        start_ref, *piece_refs, held_ref, sums_ref = refs
        sums_ref[...] = start_ref[...]
    else:
        *refs, sums_ref, held_ref, sems = refs
        piece_refs, weight_refs = refs[:-6], refs[-6:]
        copies = [pltpu.make_async_copy(ref, held_ref.at[n], sems.at[n]) for n, ref in enumerate(weight_refs)]
        for k in range(NC):

            @pl.when(core == k)
            def _(k=k):
                for n in LOADS[k]:
                    copies[n].start()

        sums_ref[...] = jnp.zeros_like(sums_ref)
    g0, u0, g1, u1, d0, d1 = (held_ref.at[n] for n in range(6))

    def arrived(ranks):
        if not base:
            for n in ranks:
                copies[n].wait()

    def groups():
        at = base
        for ref in piece_refs:
            for i in range(0, ref.shape[0], GROUP):
                spots = [at + i + j for j in range(GROUP)]
                yield spots, jnp.concatenate([ref[i + j] for j in range(GROUP)], axis=1)
            at += ref.shape[0]

    @pl.when(core == 0)
    def _():
        arrived(LOADS[0][:4])
        for spots, left in groups():
            for n, pair in enumerate((((0, g0), (1, u0)), ((3, g1), (4, u1)))):
                right = jnp.concatenate(
                    [
                        jnp.concatenate([read_block(maps_ref, k, ref, p) for k, ref in pair], axis=1)
                        for p in spots
                    ],
                    axis=0,
                )
                sums_ref[:, pl.ds(n * wide, wide)] += jnp.dot(left, right, preferred_element_type=F32)
        arrived(LOADS[0][4:])

    @pl.when(core == 1)
    def _():
        arrived(LOADS[1][:2])
        for spots, left in groups():
            right = jnp.concatenate(
                [
                    jnp.concatenate([read_block(maps_ref, k, ref, p) for p in spots], axis=1)
                    for k, ref in ((2, d0), (5, d1))
                ],
                axis=0,
            )
            sums_ref[:, pl.ds(0, wide)] += contract_last(left, right)
        arrived(LOADS[1][2:])


def outer_kernel(maps_ref, mine_ref, theirs_ref, held_ref, *part_refs):
    core = maps_ref[6 * SLOTS]
    g0, u0, g1, u1, d0, d1 = (held_ref.at[n] for n in range(6))

    def columns(ref, n):
        return ref[:, pl.ds(n * BLOCK, BLOCK)]

    def emit(product):
        for rank, part_ref in enumerate(part_refs):

            def step(i, carry, rank=rank, part_ref=part_ref):
                spots = [i * 2 + j for j in range(2)]
                terms = product([rank * PART + p for p in spots]).astype(part_ref.dtype)
                for j, p in enumerate(spots):
                    part_ref[p] = terms[:, j * BLOCK : (j + 1) * BLOCK]
                return carry

            lax.fori_loop(0, PART // 2, step, 0, unroll=4)

    @pl.when(core == 0)
    def _():
        hidden = []
        for n in range(NC):
            gate, upper = columns(mine_ref, 2 * n), columns(mine_ref, 2 * n + 1)
            hidden.append((gate * jax.nn.sigmoid(gate) * upper).astype(BF16))
        hidden = jnp.concatenate(hidden, axis=1)

        def product(spots):
            right = jnp.concatenate(
                [
                    jnp.concatenate([read_block(maps_ref, k, ref, p) for p in spots], axis=1)
                    for k, ref in ((2, d0), (5, d1))
                ],
                axis=0,
            )
            return jnp.dot(hidden, right, preferred_element_type=F32)

        emit(product)

    @pl.when(core == 1)
    def _():
        grads = []
        for n in range(NC):
            gate, upper = columns(theirs_ref, 2 * (1 - n)), columns(theirs_ref, 2 * (1 - n) + 1)
            grad = columns(mine_ref, n)
            sigma = jax.nn.sigmoid(gate)
            grads.append((grad * upper * sigma * (1.0 + gate * (1.0 - sigma))).astype(BF16))
            grads.append((grad * gate * sigma).astype(BF16))
        grads = jnp.concatenate(grads, axis=1)

        def product(spots):
            right = jnp.concatenate(
                [
                    jnp.concatenate(
                        [read_block(maps_ref, k, ref, p) for k, ref in ((0, g0), (1, u0), (3, g1), (4, u1))],
                        axis=1,
                    )
                    for p in spots
                ],
                axis=0,
            )
            return contract_last(grads, right)

        emit(product)


def transpose_kernel(block_ref, turned_ref):
    turned_ref[...] = block_ref[...].T


def transpose(block):
    return pl.pallas_call(
        transpose_kernel,
        out_shape=jax.ShapeDtypeStruct(block.shape[::-1], block.dtype),
        compiler_params=pltpu.CompilerParams(vmem_limit_bytes=2 << 20),
    )(block)


def call(kernel, outs, flops, maps, *inputs, weights=()):
    vmem = pl.BlockSpec(memory_space=pltpu.VMEM)
    return pl.pallas_call(
        kernel,
        out_shape=outs,
        in_specs=[pl.BlockSpec(memory_space=pltpu.SMEM)]
        + [vmem] * len(inputs)
        + [pl.BlockSpec(memory_space=pltpu.HBM)] * len(weights),
        out_specs=jax.tree.map(lambda _: vmem, outs),
        scratch_shapes=[pltpu.SemaphoreType.DMA((len(weights),))] if weights else [],
        cost_estimate=pl.CostEstimate(flops=flops, bytes_accessed=1 << 24, transcendentals=1 << 15),
        compiler_params=pltpu.CompilerParams(vmem_limit_bytes=21 << 20),
    )(maps, *inputs, *(pltpu.with_memory_space_constraint(w, pltpu.HBM) for w in weights))


def body(
    tokens,
    grad_out,
    gate_blocks,
    gate_index,
    gate_count,
    up_blocks,
    up_index,
    up_count,
    down_blocks,
    down_index,
    down_count,
):
    me = lax.axis_index("tp")
    core, my_z, my_x, my_y = me & 1, (me >> 1) & 7, (me >> 4) & 1, me >> 5
    first = core == 0
    batch = tokens.shape[0]

    tokens, grad_out = tokens.T, grad_out.T
    forward = core == 1
    own, other = jnp.where(forward, tokens, grad_out), jnp.where(forward, grad_out, tokens)
    other = shift(other, "c", 1)
    block = jnp.concatenate([jnp.where(first, own, other), jnp.where(first, other, own)])
    block = transpose(block).reshape(1, batch, BLOCK)
    pieces = large_gather(small_gather(near(block), "zy"), "yz")

    lists = jnp.concatenate([gate_index, up_index, down_index])
    counts = jnp.stack([gate_count, up_count, down_count])
    lists = jnp.concatenate([lists, counts], axis=1)
    lists = jnp.concatenate([lists, shift(lists, "c", 1)])
    index, counts = lists[:, :SLOTS], lists[:, SLOTS:]
    y, x, z = ((index >> 4) - my_y) & 3, ((index >> 3) & 1) ^ my_x, ((index & 7) - my_z) & 7
    low, high = z & 3, z >> 2

    def ranked(k):
        return jnp.where(k >= 2, 5 - k, k)

    y_rank, z_rank = ranked(y), ranked(low)
    z_large = core == 1
    from_ahead = z_large & (y_rank >= 2)
    flipped = (low == 3) | ((low == 2) & jnp.logical_not(from_ahead))
    high = jnp.where(flipped, 1 - high, high)
    position = jnp.where(z_large, z_rank * RING + y_rank, y_rank * RING + z_rank) * 4 + x * 2 + high
    number = lax.broadcasted_iota(jnp.int32, (6, SLOTS, SLOTS), 2)
    places = lax.broadcasted_iota(jnp.int32, (6, SLOTS, SLOTS), 1)
    here = (position[:, None, :] == places) & (number < counts[:, :, None])
    maps = jnp.sum(jnp.where(here, number + 1, 0), axis=2) - 1
    maps = jnp.concatenate([maps.reshape(6 * SLOTS), (1 - core)[None]])

    weights = (gate_blocks, up_blocks, shift(gate_blocks, "c", 1), shift(up_blocks, "c", 1))
    weights += (down_blocks, shift(down_blocks, "c", 1))
    flops = NC * SLOTS * BLOCK * BLOCK * batch
    sums = jax.ShapeDtypeStruct((batch, 4 * BLOCK), F32)
    held = jax.ShapeDtypeStruct((6, SLOTS, BLOCK, BLOCK), BF16)
    mine, held = call(
        functools.partial(inner_kernel, 0), (sums, held), 3 * flops, maps, *pieces[:3], weights=weights
    )
    mine = call(functools.partial(inner_kernel, 6 * PART), sums, flops, maps, mine, *pieces[3:], held)
    theirs = shift(mine, "c", 1)
    parts = tuple(jax.ShapeDtypeStruct((PART, batch, BLOCK), BF16 if sent else F32) for sent in SENT)
    parts = call(outer_kernel, parts, 4 * flops, maps, mine, theirs, held)
    total = near_reduce(small_reduce(*large_reduce(parts, "yz"), "zy"))
    total = transpose(total).astype(BF16)
    low, high = jnp.split(total, 2)
    own, other = jnp.where(first, low, high), jnp.where(first, high, low)
    other = shift(other, "c", 1)
    return jnp.where(forward, own, other).T, jnp.where(forward, other, own).T


def solution(mesh):
    placed = (
        P("dp", "tp"),
        P("dp", "tp"),
        P("tp", None, None),
        P("tp", None),
        P("tp"),
        P("tp", None, None),
        P("tp", None),
        P("tp"),
        P("tp", None, None),
        P("tp", None),
        P("tp"),
    )
    return jax.shard_map(
        body, mesh=mesh, in_specs=placed, out_specs=(P("dp", "tp"), P("dp", "tp")), check_vma=False
    )
```

```python
import functools

import jax
import jax.numpy as jnp
from jax import lax
from jax.experimental import pallas as pl
from jax.experimental.pallas import tpu as pltpu
from jax.sharding import PartitionSpec as P

NY, NX, NZ, NC = 4, 2, 8, 2
SIZES = {"y": NY, "x": NX, "z": NZ, "c": NC}
BLOCK = 128
SLOTS = NY * NX * NZ
RING = 4
PIECES = 2 * RING
PART = SLOTS // PIECES
GROUP = 4
F32 = jnp.float32
BF16 = jnp.bfloat16


def permute(value, target):
    pairs = []
    for y in range(NY):
        for x in range(NX):
            for z in range(NZ):
                for c in range(NC):
                    at = {"y": y, "x": x, "z": z, "c": c}
                    to = target(dict(at))
                    numbers = [((k["y"] * NX + k["x"]) * NZ + k["z"]) * NC + k["c"] for k in (at, to)]
                    pairs.append(tuple(numbers))
    return lax.ppermute(value, "tp", pairs)


def shift(value, axis, step):
    def target(at):
        at[axis] = (at[axis] + step) % SIZES[axis]
        return at

    return permute(value, target)


def turn(value, axes, step):
    def target(at):
        axis = axes[at["c"]]
        at[axis] = (at[axis] + step) % SIZES[axis]
        return at

    return permute(value, target)


def near(value):
    far = permute(value, lambda at: at | {"x": 1 - at["x"], "z": (at["z"] + 4) % NZ})
    ahead, beside = shift(value, "z", 4), shift(value, "x", 1)
    return jnp.concatenate([value, ahead, beside, far])


def near_reduce(total):
    sent = total.astype(BF16)
    far = permute(sent[3], lambda at: at | {"x": 1 - at["x"], "z": (at["z"] + 4) % NZ})
    ahead, beside = shift(sent[1], "z", 4), shift(sent[2], "x", 1)
    return total[0] + ahead.astype(F32) + beside.astype(F32) + far.astype(F32)


def small_gather(value, axes):
    up, down = turn(value, axes, 1), turn(value, axes, -1)
    return jnp.concatenate([value, down, up, turn(up, axes, 1)])


def large_gather(value, axes):
    half = value.shape[0] // 2
    up, down = turn(value, axes, 1), turn(value, axes, -1)
    return value, down, up, turn(pick(up, 0, half), axes, 1), turn(pick(down, half, half), axes, -1)


def pick(blocks, start, count):
    def kernel(blocks_ref, picked_ref):
        picked_ref[...] = blocks_ref[start : start + count]

    return pl.pallas_call(
        kernel,
        out_shape=jax.ShapeDtypeStruct((count, *blocks.shape[1:]), blocks.dtype),
        compiler_params=pltpu.CompilerParams(vmem_limit_bytes=4 << 20),
    )(blocks)


SENT = (False, False, True, False, False, True, True, True)


def large_reduce(parts, axes):
    first, second, first_ahead, second_ahead, first_behind, second_behind, first_far, second_far = parts
    second_far, first_far = turn(second_far, axes, 1), turn(first_far, axes, -1)
    first_ahead, second_behind = turn(first_ahead, axes, 1), turn(second_behind, axes, -1)
    second_ahead = turn((second_ahead + second_far.astype(F32)).astype(BF16), axes, 1)
    first_behind = turn((first_behind + first_far.astype(F32)).astype(BF16), axes, -1)
    first = first + first_ahead.astype(F32) + first_behind.astype(F32)
    second = second + second_ahead.astype(F32) + second_behind.astype(F32)
    return first, second


def small_reduce(first, second, axes):
    here, ahead = jnp.split(first, 2)
    behind, far = jnp.split(second, 2)
    far = turn(far.astype(BF16), axes, -1)
    ahead = turn(ahead.astype(BF16), axes, 1)
    behind = turn((behind + far.astype(F32)).astype(BF16), axes, -1)
    return here + ahead.astype(F32) + behind.astype(F32)


def read_block(maps_ref, which, blocks_ref, position):
    slot = maps_ref[which * SLOTS + position]
    return jnp.where(slot >= 0, blocks_ref[jnp.maximum(slot, 0)], jnp.zeros((), BF16))


def contract_last(left, right):
    return lax.dot_general(left, right, (((1,), (1,)), ((), ())), preferred_element_type=F32)


LOADS = ((0, 1, 2, 3, 4, 5), (4, 5, 0, 1, 2, 3))


def inner_kernel(base, maps_ref, *refs):
    core = maps_ref[6 * SLOTS]
    wide = 2 * BLOCK
    if base:
        start_ref, *piece_refs, held_ref, sums_ref = refs
        sums_ref[...] = start_ref[...]
    else:
        *refs, sums_ref, held_ref, sems = refs
        piece_refs, weight_refs = refs[:-6], refs[-6:]
        copies = [pltpu.make_async_copy(ref, held_ref.at[n], sems.at[n]) for n, ref in enumerate(weight_refs)]
        for k in range(NC):

            @pl.when(core == k)
            def _(k=k):
                for n in LOADS[k]:
                    copies[n].start()

        sums_ref[...] = jnp.zeros_like(sums_ref)
    g0, u0, g1, u1, d0, d1 = (held_ref.at[n] for n in range(6))

    def arrived(ranks):
        if not base:
            for n in ranks:
                copies[n].wait()

    def groups():
        at = base
        for ref in piece_refs:
            for i in range(0, ref.shape[0], GROUP):
                spots = [at + i + j for j in range(GROUP)]
                yield spots, jnp.concatenate([ref[i + j] for j in range(GROUP)], axis=1)
            at += ref.shape[0]

    @pl.when(core == 0)
    def _():
        arrived(LOADS[0][:4])
        for spots, left in groups():
            for n, pair in enumerate((((0, g0), (1, u0)), ((3, g1), (4, u1)))):
                right = jnp.concatenate(
                    [
                        jnp.concatenate([read_block(maps_ref, k, ref, p) for k, ref in pair], axis=1)
                        for p in spots
                    ],
                    axis=0,
                )
                sums_ref[:, pl.ds(n * wide, wide)] += jnp.dot(left, right, preferred_element_type=F32)
        arrived(LOADS[0][4:])

    @pl.when(core == 1)
    def _():
        arrived(LOADS[1][:2])
        for spots, left in groups():
            right = jnp.concatenate(
                [
                    jnp.concatenate([read_block(maps_ref, k, ref, p) for p in spots], axis=1)
                    for k, ref in ((2, d0), (5, d1))
                ],
                axis=0,
            )
            sums_ref[:, pl.ds(0, wide)] += contract_last(left, right)
        arrived(LOADS[1][2:])


def outer_kernel(maps_ref, mine_ref, theirs_ref, held_ref, *part_refs):
    core = maps_ref[6 * SLOTS]
    g0, u0, g1, u1, d0, d1 = (held_ref.at[n] for n in range(6))

    def columns(ref, n):
        return ref[:, pl.ds(n * BLOCK, BLOCK)]

    def emit(product):
        for rank, part_ref in enumerate(part_refs):

            def step(i, carry, rank=rank, part_ref=part_ref):
                spots = [i * 2 + j for j in range(2)]
                terms = product([rank * PART + p for p in spots]).astype(part_ref.dtype)
                for j, p in enumerate(spots):
                    part_ref[p] = terms[:, j * BLOCK : (j + 1) * BLOCK]
                return carry

            lax.fori_loop(0, PART // 2, step, 0, unroll=4)

    @pl.when(core == 0)
    def _():
        hidden = []
        for n in range(NC):
            gate, upper = columns(mine_ref, 2 * n), columns(mine_ref, 2 * n + 1)
            hidden.append((gate * jax.nn.sigmoid(gate) * upper).astype(BF16))
        hidden = jnp.concatenate(hidden, axis=1)

        def product(spots):
            right = jnp.concatenate(
                [
                    jnp.concatenate([read_block(maps_ref, k, ref, p) for p in spots], axis=1)
                    for k, ref in ((2, d0), (5, d1))
                ],
                axis=0,
            )
            return jnp.dot(hidden, right, preferred_element_type=F32)

        emit(product)

    @pl.when(core == 1)
    def _():
        grads = []
        for n in range(NC):
            gate, upper = columns(theirs_ref, 2 * (1 - n)), columns(theirs_ref, 2 * (1 - n) + 1)
            grad = columns(mine_ref, n)
            sigma = jax.nn.sigmoid(gate)
            grads.append((grad * upper * sigma * (1.0 + gate * (1.0 - sigma))).astype(BF16))
            grads.append((grad * gate * sigma).astype(BF16))
        grads = jnp.concatenate(grads, axis=1)

        def product(spots):
            right = jnp.concatenate(
                [
                    jnp.concatenate(
                        [read_block(maps_ref, k, ref, p) for k, ref in ((0, g0), (1, u0), (3, g1), (4, u1))],
                        axis=1,
                    )
                    for p in spots
                ],
                axis=0,
            )
            return contract_last(grads, right)

        emit(product)


def transpose_kernel(block_ref, turned_ref):
    turned_ref[...] = block_ref[...].T


def transpose(block):
    return pl.pallas_call(
        transpose_kernel,
        out_shape=jax.ShapeDtypeStruct(block.shape[::-1], block.dtype),
        compiler_params=pltpu.CompilerParams(vmem_limit_bytes=2 << 20),
    )(block)


def call(kernel, outs, flops, maps, *inputs, weights=()):
    vmem = pl.BlockSpec(memory_space=pltpu.VMEM)
    return pl.pallas_call(
        kernel,
        out_shape=outs,
        in_specs=[pl.BlockSpec(memory_space=pltpu.SMEM)]
        + [vmem] * len(inputs)
        + [pl.BlockSpec(memory_space=pltpu.HBM)] * len(weights),
        out_specs=jax.tree.map(lambda _: vmem, outs),
        scratch_shapes=[pltpu.SemaphoreType.DMA((len(weights),))] if weights else [],
        cost_estimate=pl.CostEstimate(flops=flops, bytes_accessed=1 << 24, transcendentals=1 << 15),
        compiler_params=pltpu.CompilerParams(vmem_limit_bytes=21 << 20),
    )(maps, *inputs, *(pltpu.with_memory_space_constraint(w, pltpu.HBM) for w in weights))


def body(
    tokens,
    grad_out,
    gate_blocks,
    gate_index,
    gate_count,
    up_blocks,
    up_index,
    up_count,
    down_blocks,
    down_index,
    down_count,
):
    me = lax.axis_index("tp")
    core, my_z, my_x, my_y = me & 1, (me >> 1) & 7, (me >> 4) & 1, me >> 5
    first = core == 0
    batch = tokens.shape[0]

    tokens, grad_out = tokens.T, grad_out.T
    own, other = jnp.where(first, tokens, grad_out), jnp.where(first, grad_out, tokens)
    other = shift(other, "c", 1)
    block = jnp.concatenate([jnp.where(first, own, other), jnp.where(first, other, own)])
    block = transpose(block).reshape(1, batch, BLOCK)
    pieces = large_gather(small_gather(near(block), "zy"), "yz")

    lists = jnp.concatenate([gate_index, up_index, down_index])
    counts = jnp.stack([gate_count, up_count, down_count])
    lists = jnp.concatenate([lists, counts], axis=1)
    lists = jnp.concatenate([lists, shift(lists, "c", 1)])
    index, counts = lists[:, :SLOTS], lists[:, SLOTS:]
    y, x, z = ((index >> 4) - my_y) & 3, ((index >> 3) & 1) ^ my_x, ((index & 7) - my_z) & 7
    low, high = z & 3, z >> 2

    def ranked(k):
        return jnp.where(k >= 2, 5 - k, k)

    y_rank, z_rank = ranked(y), ranked(low)
    z_large = core == 1
    from_ahead = z_large & (y_rank >= 2)
    flipped = (low == 3) | ((low == 2) & jnp.logical_not(from_ahead))
    high = jnp.where(flipped, 1 - high, high)
    position = jnp.where(z_large, z_rank * RING + y_rank, y_rank * RING + z_rank) * 4 + x * 2 + high
    number = lax.broadcasted_iota(jnp.int32, (6, SLOTS, SLOTS), 2)
    places = lax.broadcasted_iota(jnp.int32, (6, SLOTS, SLOTS), 1)
    here = (position[:, None, :] == places) & (number < counts[:, :, None])
    maps = jnp.sum(jnp.where(here, number + 1, 0), axis=2) - 1
    maps = jnp.concatenate([maps.reshape(6 * SLOTS), core[None]])

    weights = (gate_blocks, up_blocks, shift(gate_blocks, "c", 1), shift(up_blocks, "c", 1))
    weights += (down_blocks, shift(down_blocks, "c", 1))
    flops = NC * SLOTS * BLOCK * BLOCK * batch
    sums = jax.ShapeDtypeStruct((batch, 4 * BLOCK), F32)
    held = jax.ShapeDtypeStruct((6, SLOTS, BLOCK, BLOCK), BF16)
    mine, held = call(
        functools.partial(inner_kernel, 0), (sums, held), 3 * flops, maps, *pieces[:3], weights=weights
    )
    mine = call(functools.partial(inner_kernel, 6 * PART), sums, flops, maps, mine, *pieces[3:], held)
    theirs = shift(mine, "c", 1)
    parts = tuple(jax.ShapeDtypeStruct((PART, batch, BLOCK), BF16 if sent else F32) for sent in SENT)
    parts = call(outer_kernel, parts, 4 * flops, maps, mine, theirs, held)
    total = near_reduce(small_reduce(*large_reduce(parts, "yz"), "zy"))
    total = transpose(total).astype(BF16)
    low, high = jnp.split(total, 2)
    own, other = jnp.where(first, low, high), jnp.where(first, high, low)
    other = shift(other, "c", 1)
    return jnp.where(first, own, other).T, jnp.where(first, other, own).T


def solution(mesh):
    placed = (
        P("dp", "tp"),
        P("dp", "tp"),
        P("tp", None, None),
        P("tp", None),
        P("tp"),
        P("tp", None, None),
        P("tp", None),
        P("tp"),
        P("tp", None, None),
        P("tp", None),
        P("tp"),
    )
    return jax.shard_map(
        body, mesh=mesh, in_specs=placed, out_specs=(P("dp", "tp"), P("dp", "tp")), check_vma=False
    )
```
